256 devices in a mesh: subj: 4 (over z_hi, core), slab: 64 (over z_lo, y, x).
Axes of the slice: x: 4, y: 4, z: 8 (z_hi: 2, z_lo: 4; z = z_hi * 4 + z_lo), core: 2. Of those that a mesh axis runs over, the one named last changes fastest.
Arguments:
- image: bfloat16 [4, 20, 64, 2, 320], P('subj', None, 'slab'), may hold values from -6 to 6
- upstream: float32 [4, 20, 64, 2, 320], P('subj', None, 'slab'), may hold values from -6 to 6
- coil_maps: float32 [4, 2, 8, 64, 2, 320], P('subj', None, None, 'slab'), may hold values from -1.5 to 1.5
- kernel: float32 [10, 10, 64, 2, 320], P(None, None, None, None, 'slab'), may hold values from -0.5 to 5.5, as said below
- w_first: bfloat16 [3, 3, 3, 64, 20], replicated, may hold values from -0.25 to 0.25
- w_second: bfloat16 [3, 3, 3, 64, 64], replicated, may hold values from -0.15625 to 0.15625
- w_third: bfloat16 [3, 3, 3, 64, 64], replicated, may hold values from -0.15625 to 0.15625
- w_fourth: bfloat16 [3, 3, 3, 64, 64], replicated, may hold values from -0.15625 to 0.15625
- w_last: bfloat16 [3, 3, 3, 20, 64], replicated, may hold values from -0.15625 to 0.15625
Outputs:
- image_grad: float32 [4, 20, 64, 2, 320], P('subj', None, 'slab')
- w_first_grad: float32 [3, 3, 3, 64, 20], replicated
- w_second_grad: float32 [3, 3, 3, 64, 64], replicated
- w_third_grad: float32 [3, 3, 3, 64, 64], replicated
- w_fourth_grad: float32 [3, 3, 3, 64, 64], replicated
- w_last_grad: float32 [3, 3, 3, 20, 64], replicated
The draws below stay inside these ranges and needn't reach their ends.
Inputs may be any that keep to these rules, and one draw needn't show every extreme that they name: kernel[:, :, kz, x, ky] is a symmetric positive definite 10 x 10 matrix at every k-space point.
All inputs are finite; a program needn't handle non-finite values.
Results may differ from the reference program's by a relative error of at most 0.014.
Values may be sent and summed in bfloat16 or wider, within the bound.
A program may use at most 128 MiB of HBM per device.

```python
import math
import jax
import jax.numpy as jnp
from jax import lax

R = 10
COILS = 8
HID = 64
NY = 320
XW = 2
NZ = 64
SUBJ = 4
CH = 20
CELLS = 163840


def draw_kernel(key, part):
    key = jax.random.fold_in(key, 7)
    diag_key, mix_key = jax.random.split(key)
    low, high = (0.5, 2.0)
    diagonal = jnp.exp(jax.random.uniform(diag_key, (R, NZ, XW, NY), jnp.float32, jnp.log(low), jnp.log(high)))
    mixing = jax.random.uniform(mix_key, (R, R, NZ, XW, NY), jnp.float32, -1.0, 1.0)
    mixing = (mixing + jnp.swapaxes(mixing, 0, 1)) * 0.5 * 0.08
    identity = (jnp.arange(R)[:, None] == jnp.arange(R)[None, :]).astype(jnp.float32)
    identity = identity[:, :, None, None, None]
    base = identity + mixing * (1.0 - identity)
    root = jnp.sqrt(diagonal)
    return base * root[:, None] * root[None, :]


def levels(own_key, extent, pieces, smallest, top_value):
    level, own = 1.0, jax.random.fold_in(own_key, 6)
    for position, blocks in pieces:
        draws = jnp.exp(jax.random.uniform(jax.random.fold_in(own, position), (blocks,), jnp.float32, smallest / len(pieces), top_value / len(pieces)))
        level = level * jnp.repeat(draws, extent[position] // blocks).reshape([-1 if axis == position else 1 for axis in range(len(extent))])
    return level


def noise(rng, shape, deviation, reach, shards=(), kind=jnp.bfloat16):
    drawn = jax.random.normal(rng, shape, jnp.float32) * deviation
    if len(shards) > 0:
        drawn = levels(rng, shape, shards, -0.22, 0.18) * drawn
    return jnp.clip(drawn, min=-reach, max=reach).astype(kind)


def setup_inputs(seed: int = 0) -> dict:
    arg_keys = jax.random.split(jax.random.key(seed), 10)
    return {
        "image": noise(arg_keys[0], (SUBJ, CH, NZ, XW, NY), 1.0, 6.0, ((0, 4), (2, 64))),
        "upstream": noise(arg_keys[1], (SUBJ, CH, NZ, XW, NY), 1.0, 6.0, ((0, 4), (2, 64)), jnp.float32),
        "coil_maps": noise(arg_keys[2], (SUBJ, 2, COILS, NZ, XW, NY), 0.25, 1.5, ((0, 4), (3, 64)), jnp.float32),
        "kernel": draw_kernel(jax.random.fold_in(arg_keys[9], 71), 0),
        "w_first": noise(arg_keys[4], (3, 3, 3, HID, CH), (27 * CH) ** -0.5, 0.25),
        "w_second": noise(arg_keys[5], (3, 3, 3, HID, HID), (27 * HID) ** -0.5, 0.15625),
        "w_third": noise(arg_keys[6], (3, 3, 3, HID, HID), (27 * HID) ** -0.5, 0.15625),
        "w_fourth": noise(arg_keys[7], (3, 3, 3, HID, HID), (27 * HID) ** -0.5, 0.15625),
        "w_last": noise(arg_keys[8], (3, 3, 3, CH, HID), (27 * HID) ** -0.5, 0.15625),
    }


ETA_STEP = 0.5
PRECISE = lax.Precision.HIGHEST

def silu_slope(pre_act):
    sigmoid = jax.nn.sigmoid(pre_act)
    return sigmoid * (1.0 + pre_act * (1.0 - sigmoid))

def offsets():
    return [(off_z, off_x, off_y) for off_z in range(3) for off_x in range(3) for off_y in range(3)]

def conv_apply(inputs, weight, transpose):
    wide = weight.astype(jnp.float32)
    count_z, count_x, count_y = (inputs.shape[1], inputs.shape[2], inputs.shape[3])
    padded = jnp.pad(inputs.astype(jnp.float32), ((0, 0), (1, 1), (1, 1), (1, 1)))
    outputs = weight.shape[4] if transpose else weight.shape[3]
    total = jnp.zeros((outputs, count_z, count_x, count_y), jnp.float32)
    for off_z, off_x, off_y in offsets():
        if transpose:
            window = padded[:, 2 - off_z:2 - off_z + count_z, 2 - off_x:2 - off_x + count_x, 2 - off_y:2 - off_y + count_y]
            total = total + jnp.einsum('oi,ozxy->izxy', wide[off_z, off_x, off_y], window)
        else:
            window = padded[:, off_z:off_z + count_z, off_x:off_x + count_x, off_y:off_y + count_y]
            total = total + jnp.einsum('oi,izxy->ozxy', wide[off_z, off_x, off_y], window)
    return total

def weight_term(delta_grad, inputs):
    wide_delta = delta_grad.astype(jnp.float32)
    count_z, count_x, count_y = (inputs.shape[1], inputs.shape[2], inputs.shape[3])
    padded = jnp.pad(inputs.astype(jnp.float32), ((0, 0), (1, 1), (1, 1), (1, 1)))
    terms = []
    for off_z, off_x, off_y in offsets():
        window = padded[:, off_z:off_z + count_z, off_x:off_x + count_x, off_y:off_y + count_y]
        terms.append(jnp.einsum('ozxy,izxy->oi', wide_delta, window))
    stacked = jnp.stack(terms)
    return stacked.reshape(3, 3, 3, stacked.shape[1], stacked.shape[2])

def normal_operator(field, maps, kernel):
    components = field.shape[0] // 2
    vector = lax.complex(field[:components], field[components:])
    sensitivity = lax.complex(maps[0], maps[1])
    coil_images = sensitivity[:, None] * vector[None]
    spectra = jnp.fft.fftn(coil_images, axes=(2, 4), norm='ortho')
    mixing = lax.complex(kernel, jnp.zeros_like(kernel))
    mixed = jnp.einsum('rszxy,cszxy->crzxy', mixing, spectra, precision=PRECISE)
    returned = jnp.fft.ifftn(mixed, axes=(2, 4), norm='ortho')
    result = lax.optimization_barrier(jnp.sum(jnp.conj(sensitivity)[:, None] * returned, axis=0))
    return jnp.concatenate((jnp.real(result), jnp.imag(result)), axis=0)

def reference(image, upstream, coil_maps, kernel, w_first, w_second, w_third, w_fourth, w_last):
    weights = [w_first, w_second, w_third, w_fourth, w_last]
    raw_sums = [jnp.zeros(weight.shape, jnp.float32) for weight in weights]
    image_grads = []
    for subject in range(SUBJ):
        activations = [image[subject]]
        pre_acts = []
        for level in range(4):
            pre_act = conv_apply(activations[-1], weights[level], False)
            pre_acts.append(pre_act)
            activations.append(jax.nn.silu(pre_act).astype(jnp.bfloat16))
        direct = upstream[subject] - ETA_STEP * normal_operator(upstream[subject], coil_maps[subject], kernel)
        delta_grad = direct.astype(jnp.bfloat16)
        back_grad = direct
        for level in (4, 3, 2, 1, 0):
            raw_sums[level] = raw_sums[level] + weight_term(delta_grad, activations[level])
            back_grad = conv_apply(delta_grad, weights[level], True)
            if level > 0:
                delta_grad = (back_grad * silu_slope(pre_acts[level - 1])).astype(jnp.bfloat16)
        image_grads.append(direct + back_grad)
    scaling = 1.0 / math.sqrt(CELLS)
    return (jnp.stack(image_grads), raw_sums[0] * scaling, raw_sums[1] * scaling, raw_sums[2] * scaling, raw_sums[3] * scaling, raw_sums[4] * scaling)
```

```python
import functools
import math

import jax
import jax.numpy as jnp
import ml_dtypes
import numpy as np
from jax import lax
from jax.experimental import pallas as pl
from jax.experimental.pallas import tpu as pltpu
from jax.sharding import PartitionSpec as P

F32 = jnp.float32
BF16 = jnp.bfloat16
MESH = pl.DeviceIdType.MESH
NN = (((1,), (0,)), ((), ()))
NT = (((1,), (1,)), ((), ()))
TN = (((0,), (0,)), ((), ()))
SLABS = 64
NY = 320
NZ = 64
CHUNK = {0: 16, 1: 32, 2: 32, 3: 32, 4: 16}


def lane_of(x, comp, coil):
    group = x * 2 + coil // 4
    base = group * 40 if group < 3 else 128
    return base + comp * 4 + coil % 4


def slot_block(q, j):
    if q < 5:
        return q, j // 2
    if q == 5:
        return j, 1
    return min(3 + j, 4), 1


@functools.lru_cache(None)
def tables():
    half = ml_dtypes.bfloat16
    expand_u = np.zeros((512, 40), np.float32)
    expand_s = np.zeros((512, 32), np.float32)
    collect = np.zeros((512, 128), np.float32)
    for x in range(2):
        for comp in range(10):
            for coil in range(8):
                lane = lane_of(x, comp, coil)
                for part in range(2):
                    expand_u[part * 256 + lane, (part * 10 + comp) * 2 + x] = 1
                    expand_s[part * 256 + lane, part * 16 + coil * 2 + x] = 1
                    collect[part * 256 + lane, x * 64 + part * 10 + comp] = 1
    y = np.arange(NY)
    angle = 2 * np.pi * ((y[:, None] * y[None, :]) % NY) / NY
    cos = (np.cos(angle) / math.sqrt(NY)).reshape(SLABS, 5, NY)
    sin = (np.sin(angle) / math.sqrt(NY)).reshape(SLABS, 5, NY)
    rows = np.zeros((SLABS, 16, 2, 384), np.float32)
    rows[:, 0:10:2, 0, :NY] = cos
    rows[:, 0:10:2, 1, :NY] = sin
    rows[:, 1:10:2, 0, :NY] = -sin
    rows[:, 1:10:2, 1, :NY] = cos
    rows = rows.reshape(1024, 768)
    rows_back = np.zeros((2, NY, SLABS, 16), np.float32)
    cos_t, sin_t = np.moveaxis(cos, 2, 0), np.moveaxis(sin, 2, 0)
    rows_back[0, :, :, 0:10:2] = cos_t
    rows_back[0, :, :, 1:10:2] = -sin_t
    rows_back[1, :, :, 0:10:2] = sin_t
    rows_back[1, :, :, 1:10:2] = cos_t
    rows_back = rows_back.reshape(640, 1024)
    z = np.arange(NZ)
    angle = 2 * np.pi * ((z[:, None] * z[None, :]) % NZ) / NZ
    cos, sin = np.cos(angle) / 8, np.sin(angle) / 8
    depth = np.zeros((7, 2, NZ, NZ, 16), np.float32)
    depth_back = np.zeros((NZ, 16, 7, 2, NZ), np.float32)
    for q in range(7):
        depth[q, 0, :, :, 2 * q] = cos
        depth[q, 0, :, :, 2 * q + 1] = sin
        depth[q, 1, :, :, 2 * q] = -sin
        depth[q, 1, :, :, 2 * q + 1] = cos
        depth_back[:, 2 * q, q, 0] = cos
        depth_back[:, 2 * q, q, 1] = -sin
        depth_back[:, 2 * q + 1, q, 0] = sin
        depth_back[:, 2 * q + 1, q, 1] = cos
    depth = depth.reshape(896, 1024)
    depth_back = depth_back.reshape(1024, 896)
    spread = np.zeros((384, 20, 128), np.float32)
    for shift in range(-9, 10):
        for j in range(3):
            for comp in range(10):
                other = comp + shift
                if 0 <= other < 10:
                    first = j * 40 + comp * 4
                    spread[j * 128 + comp * 10 + other, shift + 9, first : first + 4] = 1
    spread = spread.reshape(384, 2560)
    out = (expand_u, expand_s, collect, rows, rows_back, depth, depth_back, spread)
    return tuple(t.astype(half) for t in out)


def dot(a, b, dims=NN):
    return lax.dot_general(a, b, dims, preferred_element_type=F32)


def shifted(block, step):
    count = block.shape[0]
    row = lax.broadcasted_iota(jnp.int32, block.shape, 0)
    rolled = pltpu.roll(block, step % count, 0)
    keep = row >= step if step > 0 else row < count + step
    return jnp.where(keep, rolled, 0.0)


def main_kernel(
    u_ref, s_ref, up_ref, image_ref, taps_ref, kt_ref, eu_ref, es_ref, eo_ref,
    rows_hbm, rows_back_hbm, depth_hbm, depth_back_hbm, spread_hbm,
    grad_ref, sums_mid_ref, sums_small_ref,
    rows_t, rows_back_t, depth_t, depth_back_t, spread_t,
    coil, maps, message, arrived, mixed, message_back, returned, unpacked, coefs, direct,
    acts, pres, deltas, parts_mid, parts_small, gathered_mid, gathered_small,
    own_mid, own_small, across_mid, across_small, total_mid, total_small,
    table_sem, send_sem, recv_sem, halo_send, halo_recv, sum_send, sum_recv,
):
    subj = lax.axis_index("subj")
    slab = lax.axis_index("slab")
    z_hi, core = subj // 2, subj % 2
    z_lo, place = slab // 16, slab % 16
    plane_index = core * 16 + place
    depth_index = z_hi * 4 + z_lo

    def slab_peer(step):
        return (subj, lax.rem(slab + step, SLABS))

    def plane_peer(step):
        other = lax.rem(plane_index + step, 32)
        return other, (z_hi * 2 + other // 16, z_lo * 16 + other % 16)

    def depth_peer(step):
        other = lax.rem(depth_index + step, 8)
        return other, ((other // 4) * 2 + core, (other % 4) * 16 + place)

    barrier = pltpu.get_barrier_semaphore()

    def greet(device):
        pl.semaphore_signal(barrier, inc=1, device_id=device, device_id_type=MESH)

    @pl.loop(1, SLABS)
    def _(step):
        greet(slab_peer(step))

    @pl.loop(0, 16)
    def _(other):
        greet((z_hi * 2 + 1 - core, z_lo * 16 + other))

    @pl.loop(0, 4)
    def _(other):
        greet(((1 - z_hi) * 2 + core, other * 16 + place))

    fetches = [
        pltpu.make_async_copy(source, target, table_sem.at[i])
        for i, (source, target) in enumerate(
            (
                (rows_hbm, rows_t),
                (spread_hbm, spread_t),
                (depth_hbm, depth_t),
                (depth_back_hbm, depth_back_t),
                (rows_back_hbm, rows_back_t),
            )
        )
    ]
    for fetch in fetches:
        fetch.start()

    zero_plane = jnp.zeros((NY, 128), BF16)
    for side, edge in ((0, 0), (2, SLABS - 1)):

        @pl.when(slab == edge)
        def _(side=side):
            for level in range(5):
                for buffers in (acts, deltas):
                    buffers[level, side] = zero_plane

    for i in range(3):
        parts_mid[i, 28:32] = jnp.zeros((4, 32, 128), BF16)
    for i in range(2):
        parts_small[i, 21:32] = jnp.zeros((11, 16, 128), BF16)
    acts[0, 1] = image_ref[...]

    def halo_copies(buffers, base, level):
        index = base + level
        up = pltpu.make_async_remote_copy(
            buffers.at[level, 1], buffers.at[level, 0],
            halo_send.at[index, 0], halo_recv.at[index, 0],
            (subj, jnp.minimum(slab + 1, SLABS - 1)), MESH,
        )
        down = pltpu.make_async_remote_copy(
            buffers.at[level, 1], buffers.at[level, 2],
            halo_send.at[index, 1], halo_recv.at[index, 1],
            (subj, jnp.maximum(slab - 1, 0)), MESH,
        )
        return up, down

    def halo_start(buffers, base, level):
        up, down = halo_copies(buffers, base, level)

        @pl.when(slab < SLABS - 1)
        def _():
            up.start()

        @pl.when(slab > 0)
        def _():
            down.start()

    def halo_wait(buffers, base, level):
        up, down = halo_copies(buffers, base, level)

        @pl.when(slab < SLABS - 1)
        def _():
            up.wait_send()
            down.wait_recv()

        @pl.when(slab > 0)
        def _():
            down.wait_send()
            up.wait_recv()

    def exchange_start(source, target, which):
        @pl.loop(1, SLABS)
        def _(step):
            subject, other = slab_peer(step)
            pltpu.make_async_remote_copy(
                source.at[other], target.at[slab], send_sem.at[which], recv_sem.at[which],
                (subject, other), MESH,
            ).start()

        target[slab] = source[slab]

    def bulk_wait(buffer, count, semaphore):
        piece = buffer.at[pl.ds(0, count)]
        pltpu.make_async_copy(piece, piece, semaphore).wait()

    def exchange_wait(source, target, which):
        bulk_wait(source, SLABS - 1, send_sem.at[which])
        bulk_wait(target, SLABS - 1, recv_sem.at[which])

    wide_u = dot(eu_ref[...], u_ref[...])
    wide_s = dot(es_ref[...], s_ref[...])
    u_re, u_im = wide_u[:256], wide_u[256:]
    s_re, s_im = wide_s[:256], wide_s[256:]
    coil[...] = jnp.zeros((256, 768), BF16)
    coil[:, 0:NY] = (s_re * u_re - s_im * u_im).astype(BF16)
    coil[:, 384 : 384 + NY] = (s_re * u_im + s_im * u_re).astype(BF16)
    maps[...] = dot(s_ref[...], es_ref[...], (((0,), (1,)), ((), ())))
    fetches[0].wait()
    sub = lax.broadcasted_iota(jnp.int32, (8, 8, 128), 1) // 2

    @pl.loop(0, 8)
    def _(step):
        first = pl.multiple_of(step * 128, 128)
        spectra = dot(rows_t[pl.ds(first, 128), :], coil[...], NT)
        body = spectra[:, :128].reshape(8, 2, 8, 128)
        rest = spectra[:, 128:].reshape(8, 2, 8, 128)
        low, high = rest[:, 0], rest[:, 1]
        lowered = pltpu.roll(low, 6, 1)
        at_one = pltpu.roll(low, 2, 1) + pltpu.roll(low, 40, 2) + pltpu.roll(lowered, 80, 2)
        at_two = lowered + pltpu.roll(pltpu.roll(high, 4, 1), 40, 2)
        extra = jnp.where(sub == 1, at_one, jnp.where(sub == 2, at_two, 0.0))
        packed = jnp.concatenate([body[:, 0:1], (body[:, 1] + extra)[:, None]], axis=1)
        message[pl.ds(step * 8, 8)] = packed.reshape(8, 16, 128).astype(BF16)

    pl.semaphore_wait(barrier, 83)
    halo_start(acts, 0, 0)
    exchange_start(message, arrived, 0)

    def forward(level):
        taps = taps_ref[level]
        wide = [taps[3 * k : 3 * k + 3].reshape(384, 128) for k in range(3)]
        spread_out = dot(acts[level, 1], wide[1], NT)
        halo_wait(acts, 0, level)
        sides = jnp.concatenate([acts[level, 0], acts[level, 2]], axis=1)
        spread_out += dot(sides, jnp.concatenate([wide[0], wide[2]], axis=1), NT)
        pre = (
            shifted(spread_out[:, :128], 1)
            + spread_out[:, 128:256]
            + shifted(spread_out[:, 256:], -1)
        )
        pres[level] = pre
        acts[level + 1, 1] = (pre * jax.nn.sigmoid(pre)).astype(BF16)
        halo_start(acts, 0, level + 1)

    fetches[1].wait()
    blocks = []
    for q in range(7):
        picks = [slot_block(q, j) for j in range(3)]
        blocks.append(jnp.concatenate([kt_ref[ky * 2 + x] for ky, x in picks], axis=1))
    stacked = jnp.concatenate(blocks, axis=0)
    for step in range(10):
        pair = dot(stacked, spread_t[:, step * 256 : step * 256 + 256])
        coefs[2 * step] = pair[:, :128]
        if step < 9:
            coefs[2 * step + 1] = pair[:, 128:]
    forward(0)
    forward(1)

    fetches[2].wait()
    fetches[3].wait()
    exchange_wait(message, arrived, 0)

    @pl.loop(0, 7)
    def _(q):
        first = pl.multiple_of(q * 128, 128)
        spectrum = dot(depth_t[pl.ds(first, 128), :], arrived[...].reshape(1024, 128))
        real, imag = spectrum[:64], spectrum[64:]
        out_real = jnp.zeros((64, 128), F32)
        out_imag = jnp.zeros((64, 128), F32)
        for shift in range(-9, 10):
            factor = coefs[shift + 9, pl.ds(pl.multiple_of(q * 64, 64), 64), :]
            turn = (-4 * shift) % 128
            moved_real = real if turn == 0 else pltpu.roll(real, turn, 1)
            moved_imag = imag if turn == 0 else pltpu.roll(imag, turn, 1)
            out_real += factor * moved_real
            out_imag += factor * moved_imag
        mixed[pl.ds(first, 64), :] = out_real.astype(BF16)
        mixed[pl.ds(first + 64, 64), :] = out_imag.astype(BF16)

    @pl.loop(0, 8)
    def _(step):
        first = pl.multiple_of(step * 128, 128)
        back = dot(depth_back_t[pl.ds(first, 128), :], mixed[...])
        message_back[pl.ds(step * 8, 8)] = back.astype(BF16).reshape(8, 16, 128)

    exchange_start(message_back, returned, 1)
    forward(2)
    forward(3)
    halo_wait(acts, 0, 4)
    exchange_wait(message_back, returned, 1)

    @pl.loop(0, 8)
    def _(step):
        block = returned[pl.ds(step * 8, 8)].astype(F32)
        body = block.reshape(8, 2, 8, 128)[:, 1]
        raised = pltpu.roll(body, 2, 1)
        low = jnp.where(
            sub == 0,
            pltpu.roll(body, 6, 1),
            jnp.where(
                sub == 1,
                pltpu.roll(body, 88, 2),
                jnp.where(sub == 2, pltpu.roll(raised, 48, 2), raised),
            ),
        )
        high = jnp.where(sub == 0, pltpu.roll(pltpu.roll(body, 4, 1), 88, 2), 0.0)
        rest = jnp.concatenate([low[:, None], high[:, None]], axis=1).reshape(128, 128)
        first = pl.multiple_of(step * 128, 128)
        unpacked[pl.ds(first, 128), 0:128] = block.reshape(128, 128).astype(BF16)
        unpacked[pl.ds(first, 128), 128:256] = rest.astype(BF16)

    fetches[4].wait()
    back_re = dot(rows_back_t[0:NY, :], unpacked[...])
    back_im = dot(rows_back_t[NY:, :], unpacked[...])
    s_re, s_im = maps[:, :256], maps[:, 256:]
    out_re = (s_re * back_re + s_im * back_im).astype(BF16)
    out_im = (s_re * back_im - s_im * back_re).astype(BF16)
    normal = dot(out_re, eo_ref[0:256, :]) + dot(out_im, eo_ref[256:, :])
    own_direct = up_ref[...] - 0.5 * normal
    direct[...] = own_direct
    deltas[4, 1] = own_direct.astype(BF16)

    def buffers_of(level):
        if level in (0, 4):
            i = level // 4
            return [
                b.at[i]
                for b in (parts_small, gathered_small, own_small, across_small, total_small)
            ]
        return [
            b.at[level - 1] for b in (parts_mid, gathered_mid, own_mid, across_mid, total_mid)
        ]

    def sum_scatter(level):
        parts, gathered, _, _, _ = buffers_of(level)

        @pl.loop(1, 32)
        def _(step):
            other, device = plane_peer(step)
            pltpu.make_async_remote_copy(
                parts.at[other], gathered.at[plane_index],
                sum_send.at[level, 0], sum_recv.at[level, 0], device, MESH,
            ).start()

        gathered[plane_index] = parts[plane_index]

    def sum_across(level):
        parts, gathered, own, across, _ = buffers_of(level)
        bulk_wait(parts, 31, sum_send.at[level, 0])
        bulk_wait(gathered, 31, sum_recv.at[level, 0])
        own[0] = jnp.sum(gathered[...].astype(F32), axis=0).astype(BF16)

        @pl.loop(1, 8)
        def _(step):
            _, device = depth_peer(step)
            pltpu.make_async_remote_copy(
                own.at[0], across.at[depth_index],
                sum_send.at[level, 1], sum_recv.at[level, 1], device, MESH,
            ).start()

        across[depth_index] = own[0]

    def sum_spread(level):
        _, _, own, across, total = buffers_of(level)
        bulk_wait(across, 7, sum_send.at[level, 1])
        bulk_wait(across, 7, sum_recv.at[level, 1])
        total[plane_index] = jnp.sum(across[...].astype(F32), axis=0).astype(BF16)

        @pl.loop(1, 32)
        def _(step):
            _, device = plane_peer(step)
            pltpu.make_async_remote_copy(
                total.at[plane_index], total.at[plane_index],
                sum_send.at[level, 2], sum_recv.at[level, 2], device, MESH,
            ).start()

    def sum_finish(level):
        total = buffers_of(level)[4]
        bulk_wait(total, 31, sum_send.at[level, 2])
        bulk_wait(total, 31, sum_recv.at[level, 2])
        if level in (0, 4):
            sums_small_ref[level // 4] = total[...].reshape(512, 128)
        else:
            sums_mid_ref[level - 1] = total[...].reshape(1024, 128)

    def weight_part(level, delta):
        parts = buffers_of(level)[0]
        moved = jnp.concatenate(
            [shifted(delta, -1), delta, shifted(delta, 1)], axis=1
        ).astype(BF16)
        inputs = jnp.concatenate([acts[level, 0], acts[level, 1], acts[level, 2]], axis=1)
        if level == 0:
            raw = dot(inputs, moved, TN)
        else:
            raw = dot(moved, inputs, TN)
        count = 24 if level in (0, 4) else 64
        lane = lax.broadcasted_iota(jnp.int32, (count, 128), 1)
        slots, lower, turned = [], [], []
        for a in range(3):
            for b in range(3):
                first = raw[a * 128 : a * 128 + count, b * 128 : b * 128 + 128]
                second = raw[a * 128 + 64 : a * 128 + 64 + count, b * 128 : b * 128 + 128]
                roll = pltpu.roll(second, 64, 1)
                slots.append(first + jnp.where(lane < 64, roll, 0.0))
                lower.append(second)
                turned.append(roll)
        for k in range(5):
            left = lower[2 * k + 1] if k < 4 else jnp.zeros((count, 128), F32)
            slots.append(jnp.where(lane < 64, left, turned[2 * k]))
        if count == 64:
            for k in range(14):
                parts[2 * k : 2 * k + 2] = slots[k].astype(BF16).reshape(2, 32, 128)
        else:
            for k in range(7):
                both = jnp.concatenate([slots[2 * k], slots[2 * k + 1]], axis=0)
                parts[3 * k : 3 * k + 3] = both.astype(BF16).reshape(3, 16, 128)

    halo_start(deltas, 5, 4)
    delta = own_direct.astype(BF16).astype(F32)
    for level in (4, 3, 2, 1, 0):
        weight_part(level, delta)
        sum_scatter(level)
        if level + 2 < 5:
            sum_spread(level + 2)
        if level + 1 < 5:
            sum_across(level + 1)
        taps = taps_ref[level]
        wide = [
            jnp.concatenate([taps[3 * k], taps[3 * k + 1], taps[3 * k + 2]], axis=1)
            for k in (2, 1, 0)
        ]
        spread_out = dot(deltas[level, 1], wide[1])
        halo_wait(deltas, 5, level)
        sides = jnp.concatenate([deltas[level, 0], deltas[level, 2]], axis=1)
        spread_out += dot(sides, jnp.concatenate([wide[0], wide[2]], axis=0))
        back = (
            shifted(spread_out[:, :128], -1)
            + spread_out[:, 128:256]
            + shifted(spread_out[:, 256:], 1)
        )
        if level > 0:
            pre = pres[level - 1]
            sigmoid = jax.nn.sigmoid(pre)
            rounded = (back * (sigmoid * (1.0 + pre * (1.0 - sigmoid)))).astype(BF16)
            deltas[level - 1, 1] = rounded
            halo_start(deltas, 5, level - 1)
            delta = rounded.astype(F32)
        else:
            grad_ref[...] = direct[...] + back
    sum_across(0)
    sum_spread(1)
    sum_spread(0)
    for level in (4, 3, 2, 1, 0):
        sum_finish(level)


def main_call(u, s, up, image, taps, kt):
    eu, es, eo, rows, rows_back, depth, depth_back, spread = tables()
    vmem = pl.BlockSpec(memory_space=pltpu.VMEM)
    hbm = pl.BlockSpec(memory_space=pl.ANY)
    big = [rows, rows_back, depth, depth_back, spread]
    return pl.pallas_call(
        main_kernel,
        out_shape=(
            jax.ShapeDtypeStruct((NY, 128), F32),
            jax.ShapeDtypeStruct((3, 1024, 128), BF16),
            jax.ShapeDtypeStruct((2, 512, 128), BF16),
        ),
        in_specs=[vmem] * 9 + [hbm] * 5,
        out_specs=(vmem, vmem, vmem),
        scratch_shapes=[pltpu.VMEM(t.shape, BF16) for t in big]
        + [
            pltpu.VMEM((256, 768), BF16),
            pltpu.VMEM((NY, 512), F32),
            pltpu.VMEM((SLABS, 16, 128), BF16),
            pltpu.VMEM((SLABS, 16, 128), BF16),
            pltpu.VMEM((896, 128), BF16),
            pltpu.VMEM((SLABS, 16, 128), BF16),
            pltpu.VMEM((SLABS, 16, 128), BF16),
            pltpu.VMEM((1024, 256), BF16),
            pltpu.VMEM((19, 448, 128), F32),
            pltpu.VMEM((NY, 128), F32),
            pltpu.VMEM((5, 3, NY, 128), BF16),
            pltpu.VMEM((4, NY, 128), F32),
            pltpu.VMEM((5, 3, NY, 128), BF16),
            pltpu.VMEM((3, 32, 32, 128), BF16),
            pltpu.VMEM((2, 32, 16, 128), BF16),
            pltpu.VMEM((3, 32, 32, 128), BF16),
            pltpu.VMEM((2, 32, 16, 128), BF16),
            pltpu.VMEM((3, 1, 32, 128), BF16),
            pltpu.VMEM((2, 1, 16, 128), BF16),
            pltpu.VMEM((3, 8, 32, 128), BF16),
            pltpu.VMEM((2, 8, 16, 128), BF16),
            pltpu.VMEM((3, 32, 32, 128), BF16),
            pltpu.VMEM((2, 32, 16, 128), BF16),
            pltpu.SemaphoreType.DMA((5,)),
            pltpu.SemaphoreType.DMA((2,)),
            pltpu.SemaphoreType.DMA((2,)),
            pltpu.SemaphoreType.DMA((10, 2)),
            pltpu.SemaphoreType.DMA((10, 2)),
            pltpu.SemaphoreType.DMA((5, 3)),
            pltpu.SemaphoreType.DMA((5, 3)),
        ],
        compiler_params=pltpu.CompilerParams(
            collective_id=0, has_side_effects=True, vmem_limit_bytes=50 * 1024 * 1024
        ),
        cost_estimate=pl.CostEstimate(
            flops=8_000_000_000, bytes_accessed=20_000_000, transcendentals=400_000
        ),
        name="step",
    )(u, s, up, image, taps, kt, eu, es, eo, rows, rows_back, depth, depth_back, spread)


def finish_kernel(scale, mid_ref, small_ref, first_ref, second_ref, third_ref, fourth_ref, last_ref):
    def place(source, count, keep, target, tap_of):
        def rows_at(slot):
            if count == 64:
                return source[slot * 64 : slot * 64 + 64, :].astype(F32)
            start = (slot // 2) * 48
            both = source[start : start + 48, :].astype(F32)
            return both[(slot % 2) * 24 : (slot % 2) * 24 + 24]

        def left(block):
            return block[:keep, :64] * scale

        def right(block):
            return pltpu.roll(block, 64, 1)[:keep, :64] * scale

        for a in range(3):
            for b in range(3):
                block = rows_at(a * 3 + b)
                target[tap_of(a, b, 0)] = left(block)
                target[tap_of(a, b, 1)] = right(block)
        for k in range(5):
            block = rows_at(9 + k)
            target[tap_of((2 * k) // 3, (2 * k) % 3, 2)] = right(block)
            if k < 4:
                target[tap_of((2 * k + 1) // 3, (2 * k + 1) % 3, 2)] = left(block)

    def usual(a, b, kind):
        return b * 9 + (1, 2, 0)[kind] * 3 + a

    def turned(a, b, kind):
        return a * 9 + (1, 0, 2)[kind] * 3 + b

    place(small_ref.at[0], 24, 20, first_ref, turned)
    place(mid_ref.at[0], 64, 64, second_ref, usual)
    place(mid_ref.at[1], 64, 64, third_ref, usual)
    place(mid_ref.at[2], 64, 64, fourth_ref, usual)
    place(small_ref.at[1], 24, 20, last_ref, usual)


def finish_call(mid, small, cells):
    shapes = [(27, 20, 64), (27, 64, 64), (27, 64, 64), (27, 64, 64), (27, 20, 64)]
    return pl.pallas_call(
        functools.partial(finish_kernel, 1.0 / math.sqrt(cells)),
        out_shape=[jax.ShapeDtypeStruct(shape, F32) for shape in shapes],
        in_specs=[pl.BlockSpec(memory_space=pltpu.VMEM)] * 2,
        out_specs=[pl.BlockSpec(memory_space=pltpu.VMEM)] * 5,
        compiler_params=pltpu.CompilerParams(vmem_limit_bytes=24 * 1024 * 1024),
        name="finish",
    )(mid, small)


def body(image, upstream, coil_maps, kernel, w_first, w_second, w_third, w_fourth, w_last):
    u = upstream[0].reshape(40, NY).astype(BF16)
    s = coil_maps[0].reshape(32, NY).astype(BF16)

    def cells_first(block):
        turned = jnp.transpose(block, (2, 1, 0))
        return jnp.pad(turned, ((0, 0), (0, 0), (0, 44))).reshape(NY, 128)

    up = cells_first(upstream[0, :, 0])
    image_cells = cells_first(image[0, :, 0])
    first = jnp.pad(w_first, ((0, 0),) * 4 + ((0, 44),))
    last = jnp.pad(w_last, ((0, 0),) * 3 + ((0, 44), (0, 0)))
    every = jnp.stack([first, w_second, w_third, w_fourth, last])
    top = jnp.concatenate([every[:, :, 1], every[:, :, 2]], axis=-1)
    bottom = jnp.concatenate([every[:, :, 0], every[:, :, 1]], axis=-1)
    taps = jnp.concatenate([top, bottom], axis=3).reshape(5, 9, 128, 128)
    kt = jnp.transpose(kernel, (4, 3, 2, 0, 1)).astype(BF16).reshape(10, NZ, 100)
    kt = jnp.pad(kt, ((0, 0), (0, 0), (0, 28)))
    grad, mid, small = main_call(u, s, up, image_cells, taps, kt)
    cells = (
        lax.axis_size("subj") * image.shape[0] * lax.axis_size("slab") * image.shape[2] * 2 * NY
    )
    first, second, third, fourth, last = finish_call(mid, small, cells)
    image_grad = jnp.transpose(grad.reshape(NY, 2, 64)[:, :, :20], (2, 1, 0))[None, :, None]
    return (
        image_grad,
        jnp.swapaxes(first, 1, 2).reshape(3, 3, 3, 64, 20),
        second.reshape(3, 3, 3, 64, 64),
        third.reshape(3, 3, 3, 64, 64),
        fourth.reshape(3, 3, 3, 64, 64),
        last.reshape(3, 3, 3, 20, 64),
    )


def solution(mesh):
    in_specs = (
        P("subj", None, "slab", None, None),
        P("subj", None, "slab", None, None),
        P("subj", None, None, "slab", None, None),
        P(None, None, None, None, "slab"),
        P(),
        P(),
        P(),
        P(),
        P(),
    )
    out_specs = (P("subj", None, "slab", None, None), P(), P(), P(), P(), P())
    return jax.shard_map(body, mesh=mesh, in_specs=in_specs, out_specs=out_specs, check_vma=False)
```

```python
import functools
import math

import jax
import jax.numpy as jnp
import ml_dtypes
import numpy as np
from jax import lax
from jax.experimental import pallas as pl
from jax.experimental.pallas import tpu as pltpu
from jax.sharding import PartitionSpec as P

F32 = jnp.float32
BF16 = jnp.bfloat16
MESH = pl.DeviceIdType.MESH
NN = (((1,), (0,)), ((), ()))
NT = (((1,), (1,)), ((), ()))
TN = (((0,), (0,)), ((), ()))
SLABS = 64
NY = 320
NZ = 64
STEP = 8


def lane_of(x, comp, coil):
    group = x * 2 + coil // 4
    base = group * 40 if group < 3 else 128
    return base + comp * 4 + coil % 4


def slot_block(q, j):
    if q < 5:
        return q, j // 2
    if q == 5:
        return j, 1
    return min(3 + j, 4), 1


@functools.lru_cache(None)
def tables():
    half = ml_dtypes.bfloat16
    expand_u = np.zeros((512, 40), np.float32)
    expand_s = np.zeros((512, 32), np.float32)
    collect = np.zeros((512, 128), np.float32)
    for x in range(2):
        for comp in range(10):
            for coil in range(8):
                lane = lane_of(x, comp, coil)
                for part in range(2):
                    expand_u[part * 256 + lane, (part * 10 + comp) * 2 + x] = 1
                    expand_s[part * 256 + lane, part * 16 + coil * 2 + x] = 1
                    collect[part * 256 + lane, x * 64 + part * 10 + comp] = 1
    y = np.arange(NY)
    angle = 2 * np.pi * ((y[:, None] * y[None, :]) % NY) / NY
    cos = (np.cos(angle) / math.sqrt(NY)).reshape(SLABS, 5, NY)
    sin = (np.sin(angle) / math.sqrt(NY)).reshape(SLABS, 5, NY)
    rows = np.zeros((SLABS, 16, 2, 384), np.float32)
    rows[:, 0:10:2, 0, :NY] = cos
    rows[:, 0:10:2, 1, :NY] = sin
    rows[:, 1:10:2, 0, :NY] = -sin
    rows[:, 1:10:2, 1, :NY] = cos
    rows = rows.reshape(1024, 768)
    rows_back = np.zeros((2, NY, SLABS, 16), np.float32)
    cos_t, sin_t = np.moveaxis(cos, 2, 0), np.moveaxis(sin, 2, 0)
    rows_back[0, :, :, 0:10:2] = cos_t
    rows_back[0, :, :, 1:10:2] = -sin_t
    rows_back[1, :, :, 0:10:2] = sin_t
    rows_back[1, :, :, 1:10:2] = cos_t
    rows_back = rows_back.reshape(640, 1024)
    z = np.arange(NZ)
    angle = 2 * np.pi * ((z[:, None] * z[None, :]) % NZ) / NZ
    cos, sin = np.cos(angle) / 8, np.sin(angle) / 8
    depth = np.zeros((7, 2, NZ, NZ, 16), np.float32)
    depth_back = np.zeros((NZ, 16, 7, 2, NZ), np.float32)
    for q in range(7):
        depth[q, 0, :, :, 2 * q] = cos
        depth[q, 0, :, :, 2 * q + 1] = sin
        depth[q, 1, :, :, 2 * q] = -sin
        depth[q, 1, :, :, 2 * q + 1] = cos
        depth_back[:, 2 * q, q, 0] = cos
        depth_back[:, 2 * q, q, 1] = -sin
        depth_back[:, 2 * q + 1, q, 0] = sin
        depth_back[:, 2 * q + 1, q, 1] = cos
    depth = depth.reshape(896, 1024)
    depth_back = depth_back.reshape(1024, 896)
    spread = np.zeros((384, 20, 128), np.float32)
    for shift in range(-9, 10):
        for j in range(3):
            for comp in range(10):
                other = comp + shift
                if 0 <= other < 10:
                    first = j * 40 + comp * 4
                    spread[j * 128 + comp * 10 + other, shift + 9, first : first + 4] = 1
    spread = spread.reshape(384, 2560)
    out = (expand_u, expand_s, collect, rows, rows_back, depth, depth_back, spread)
    return tuple(t.astype(half) for t in out)


def dot(a, b, dims=NN):
    return lax.dot_general(a, b, dims, preferred_element_type=F32)


def main_kernel(
    u_ref, s_ref, up_ref, image_ref, w1_ref, w2_ref, w3_ref, w4_ref, w5_ref, kt_ref,
    eu_ref, es_ref, eo_ref,
    rows_hbm, rows_back_hbm, depth_hbm, depth_back_hbm, spread_hbm,
    grad_ref, sums_mid_ref, sums_small_ref,
    rows_t, rows_back_t, depth_t, depth_back_t, spread_t,
    taps_ref, coil, maps, message, arrived, mixed, message_back, returned, unpacked, coefs, direct,
    padded, stage_image, stage_delta, acts, slopes, deltas, inside, back_core, back_rows, parts_mid, parts_small, halves_mid, halves_small,
    folded_mid, folded_small, gathered_mid, gathered_small,
    own_mid, own_small, across_mid, across_small, total_mid, total_small,
    table_sem, send_sem, recv_sem, block_send, block_recv, sum_send, sum_recv,
):
    subj = lax.axis_index("subj")
    slab = lax.axis_index("slab")
    z_hi, core = subj // 2, subj % 2
    z_lo, place = slab // 16, slab % 16
    plane_index = core * 16 + place
    depth_index = z_hi * 4 + z_lo

    def slab_peer(step):
        return (subj, lax.rem(slab + step, SLABS))

    def plane_peer(step):
        other = lax.rem(place + step, 16)
        return other, (subj, z_lo * 16 + other)

    twin = (z_hi * 2 + 1 - core, slab)

    def depth_peer(step):
        other = lax.rem(depth_index + step, 8)
        return other, ((other // 4) * 2 + core, (other % 4) * 16 + place)

    z_block, y_block = slab // 8, slab % 8
    zero_planes = jnp.zeros((8, 64, 128), BF16)
    for first, edge in ((0, 0), (16, 7)):

        @pl.when(z_block == edge)
        def _(first=first):
            acts[0, first : first + 8] = zero_planes
            deltas[4, first : first + 8] = zero_planes

    barrier = pltpu.get_barrier_semaphore()

    def greet(device):
        pl.semaphore_signal(barrier, inc=1, device_id=device, device_id_type=MESH)

    @pl.loop(1, SLABS)
    def _(step):
        greet(slab_peer(step))

    greet(twin)

    @pl.loop(0, 4)
    def _(other):
        greet(((1 - z_hi) * 2 + core, other * 16 + place))

    fetches = [
        pltpu.make_async_copy(source, target, table_sem.at[i])
        for i, (source, target) in enumerate(
            (
                (rows_hbm, rows_t),
                (spread_hbm, spread_t),
                (depth_hbm, depth_t),
                (depth_back_hbm, depth_back_t),
                (rows_back_hbm, rows_back_t),
            )
        )
    ]
    fetches[0].start()

    for i in range(3):
        parts_mid[i, 28:32] = jnp.zeros((4, 32, 128), BF16)
    for i in range(2):
        parts_small[i, 21:32] = jnp.zeros((11, 16, 128), BF16)
    def cut(block, stage):
        padded[8 : 8 + NY, :] = block
        for piece in range(8):
            stage[piece] = padded[40 * piece : 40 * piece + 64, :].astype(BF16)

    padded[0:8, :] = jnp.zeros((8, 128), F32)
    padded[8 + NY :, :] = jnp.zeros((16, 128), F32)
    cut(image_ref[...].astype(F32), stage_image)

    def blocks_send(stage, target, which):
        for group, step in ((1, -1), (2, 1), (0, 0)):
            other_block = jnp.clip(z_block + step, 0, 7)
            slot = y_block + 8 - 8 * step

            @pl.when(z_block + step == other_block)
            def _():
                @pl.loop(0 if step else 1, 8)
                def _(turn):
                    piece = lax.rem(y_block + turn, 8)
                    pltpu.make_async_remote_copy(
                        stage.at[piece], target.at[slot],
                        block_send.at[which, group], block_recv.at[which, group],
                        (subj, other_block * 8 + piece), MESH,
                    ).start()

        target[y_block + 8] = stage[y_block]

    def blocks_wait(stage, target, which):
        bulk_wait(stage, 7, block_send.at[which, 0])
        bulk_wait(target, 7, block_recv.at[which, 0])

        @pl.when(z_block > 0)
        def _():
            bulk_wait(stage, 8, block_send.at[which, 1])
            bulk_wait(target, 8, block_recv.at[which, 2])

        @pl.when(z_block < 7)
        def _():
            bulk_wait(stage, 8, block_send.at[which, 2])
            bulk_wait(target, 8, block_recv.at[which, 1])

    def exchange_start(source, target, which):
        @pl.loop(1, SLABS)
        def _(step):
            subject, other = slab_peer(step)
            pltpu.make_async_remote_copy(
                source.at[other], target.at[slab], send_sem.at[which], recv_sem.at[which],
                (subject, other), MESH,
            ).start()

        target[slab] = source[slab]

    def bulk_wait(buffer, count, semaphore):
        piece = buffer.at[pl.ds(0, count)]
        pltpu.make_async_copy(piece, piece, semaphore).wait()

    def exchange_wait(source, target, which):
        bulk_wait(source, SLABS - 1, send_sem.at[which])
        bulk_wait(target, SLABS - 1, recv_sem.at[which])

    wide_u = dot(eu_ref[...], u_ref[...])
    wide_s = dot(es_ref[...], s_ref[...])
    u_re, u_im = wide_u[:256], wide_u[256:]
    s_re, s_im = wide_s[:256], wide_s[256:]
    coil[...] = jnp.zeros((256, 768), BF16)
    coil[:, 0:NY] = (s_re * u_re - s_im * u_im).astype(BF16)
    coil[:, 384 : 384 + NY] = (s_re * u_im + s_im * u_re).astype(BF16)
    maps[...] = dot(s_ref[...], es_ref[...], (((0,), (1,)), ((), ())))
    fetches[0].wait()
    for fetch in fetches[1:]:
        fetch.start()
    sub = lax.broadcasted_iota(jnp.int32, (8, 8, 128), 1) // 2

    @pl.loop(0, 8)
    def _(step):
        first = pl.multiple_of(step * 128, 128)
        spectra = dot(rows_t[pl.ds(first, 128), :], coil[...], NT)
        body = spectra[:, :128].reshape(8, 2, 8, 128)
        rest = spectra[:, 128:].reshape(8, 2, 8, 128)
        low, high = rest[:, 0], rest[:, 1]
        lowered = pltpu.roll(low, 6, 1)
        at_one = pltpu.roll(low, 2, 1) + pltpu.roll(low, 40, 2) + pltpu.roll(lowered, 80, 2)
        at_two = lowered + pltpu.roll(pltpu.roll(high, 4, 1), 40, 2)
        extra = jnp.where(sub == 1, at_one, jnp.where(sub == 2, at_two, 0.0))
        packed = jnp.concatenate([body[:, 0:1], (body[:, 1] + extra)[:, None]], axis=1)
        message[pl.ds(step * 8, 8)] = packed.reshape(8, 16, 128).astype(BF16)

    slot_z = lax.broadcasted_iota(jnp.int32, (24, 64, 128), 0) + (z_block * 8 - 8)
    slot_y = lax.broadcasted_iota(jnp.int32, (24, 64, 128), 1) + (y_block * 40 - 8)
    grid_ok = (slot_z >= 0) & (slot_z < NZ) & (slot_y >= 0) & (slot_y < NY)
    inside[...] = jnp.where(grid_ok, 1.0, 0.0)

    def three_planes(buffer, first, count):
        pieces = [buffer[first + k : first + k + count].reshape(count * 64, 128) for k in (-1, 0, 1)]
        return jnp.concatenate(pieces, axis=1)

    def ranges(low, high):
        return [(first, min(STEP, high - first)) for first in range(low, high, STEP)]

    def forward(level):
        taps = taps_ref[level]
        if level == 0:
            wide = jnp.concatenate(
                [jnp.concatenate([taps[3 * k + j] for j in range(3)], axis=1) for k in range(3)],
                axis=0,
            )
        else:
            wide = jnp.concatenate(
                [taps[3 * k : 3 * k + 3].reshape(384, 128) for k in range(3)], axis=1
            )
        for first, count in ranges(level + 1, 23 - level):
            out = dot(three_planes(acts.at[level], first, count), wide, NN if level == 0 else NT)
            rows = count * 64
            pre = (
                pltpu.roll(out[:, :128], 1, 0)
                + out[:, 128:256]
                + pltpu.roll(out[:, 256:], rows - 1, 0)
            )
            keep = inside[first : first + count].reshape(rows, 128)
            sigmoid = jax.nn.sigmoid(pre) * keep
            value = pre * sigmoid
            slope = sigmoid + value * (1.0 - jax.nn.sigmoid(pre))
            acts[level + 1, first : first + count] = value.astype(BF16).reshape(count, 64, 128)
            slopes[level, first : first + count] = slope.reshape(count, 64, 128)

    for level, w_ref in enumerate((w1_ref, w2_ref, w3_ref, w4_ref, w5_ref)):
        for tap in range(9):
            low, middle, high = [
                w_ref[(tap // 3) * 9 + off_x * 3 + tap % 3].astype(F32) for off_x in range(3)
            ]
            if level == 0:
                low, high = high, low
            pieces = [jnp.concatenate(pair, axis=1) for pair in ((middle, high), (low, middle))]
            if level in (0, 4):
                pieces = [
                    jnp.concatenate([piece, jnp.zeros((44, 128), F32)], axis=0) for piece in pieces
                ]
            taps_ref[level, tap] = jnp.concatenate(pieces, axis=0).astype(BF16)

    pl.semaphore_wait(barrier, 68)
    exchange_start(message, arrived, 0)
    blocks_send(stage_image, acts.at[0], 0)
    fetches[1].wait()
    blocks = []
    for q in range(7):
        picks = [slot_block(q, j) for j in range(3)]
        blocks.append(jnp.concatenate([kt_ref[ky * 2 + x] for ky, x in picks], axis=1))
    stacked = jnp.concatenate(blocks, axis=0)
    for step in range(10):
        pair = dot(stacked, spread_t[:, step * 256 : step * 256 + 256])
        coefs[2 * step] = pair[:, :128]
        if step < 9:
            coefs[2 * step + 1] = pair[:, 128:]
    blocks_wait(stage_image, acts.at[0], 0)
    forward(0)
    forward(1)

    fetches[2].wait()
    fetches[3].wait()
    exchange_wait(message, arrived, 0)

    @pl.loop(0, 7)
    def _(q):
        first = pl.multiple_of(q * 128, 128)
        spectrum = dot(depth_t[pl.ds(first, 128), :], arrived[...].reshape(1024, 128))
        real, imag = spectrum[:64], spectrum[64:]
        out_real = jnp.zeros((64, 128), F32)
        out_imag = jnp.zeros((64, 128), F32)
        for shift in range(-9, 10):
            factor = coefs[shift + 9, pl.ds(pl.multiple_of(q * 64, 64), 64), :]
            turn = (-4 * shift) % 128
            moved_real = real if turn == 0 else pltpu.roll(real, turn, 1)
            moved_imag = imag if turn == 0 else pltpu.roll(imag, turn, 1)
            out_real += factor * moved_real
            out_imag += factor * moved_imag
        mixed[pl.ds(first, 64), :] = out_real.astype(BF16)
        mixed[pl.ds(first + 64, 64), :] = out_imag.astype(BF16)

    @pl.loop(0, 8)
    def _(step):
        first = pl.multiple_of(step * 128, 128)
        back = dot(depth_back_t[pl.ds(first, 128), :], mixed[...])
        message_back[pl.ds(step * 8, 8)] = back.astype(BF16).reshape(8, 16, 128)

    exchange_start(message_back, returned, 1)
    forward(2)
    forward(3)
    exchange_wait(message_back, returned, 1)

    @pl.loop(0, 8)
    def _(step):
        block = returned[pl.ds(step * 8, 8)].astype(F32)
        body = block.reshape(8, 2, 8, 128)[:, 1]
        raised = pltpu.roll(body, 2, 1)
        low = jnp.where(
            sub == 0,
            pltpu.roll(body, 6, 1),
            jnp.where(
                sub == 1,
                pltpu.roll(body, 88, 2),
                jnp.where(sub == 2, pltpu.roll(raised, 48, 2), raised),
            ),
        )
        high = jnp.where(sub == 0, pltpu.roll(pltpu.roll(body, 4, 1), 88, 2), 0.0)
        rest = jnp.concatenate([low[:, None], high[:, None]], axis=1).reshape(128, 128)
        first = pl.multiple_of(step * 128, 128)
        unpacked[pl.ds(first, 128), 0:128] = block.reshape(128, 128).astype(BF16)
        unpacked[pl.ds(first, 128), 128:256] = rest.astype(BF16)

    fetches[4].wait()
    back_re = dot(rows_back_t[0:NY, :], unpacked[...])
    back_im = dot(rows_back_t[NY:, :], unpacked[...])
    s_re, s_im = maps[:, :256], maps[:, 256:]
    out_re = (s_re * back_re + s_im * back_im).astype(BF16)
    out_im = (s_re * back_im - s_im * back_re).astype(BF16)
    normal = dot(out_re, eo_ref[0:256, :]) + dot(out_im, eo_ref[256:, :])
    own_direct = up_ref[...] - 0.5 * normal
    direct[...] = own_direct
    cut(own_direct, stage_delta)
    blocks_send(stage_delta, deltas.at[4], 1)

    def buffers_of(level):
        if level in (0, 4):
            every = (
                parts_small, halves_small, folded_small, gathered_small, own_small,
                across_small, total_small,
            )
            return [buffer.at[level // 4] for buffer in every]
        every = (
            parts_mid, halves_mid, folded_mid, gathered_mid, own_mid, across_mid, total_mid,
        )
        return [buffer.at[level - 1] for buffer in every]

    def halves_copy(level):
        parts, halves = buffers_of(level)[:2]
        return pltpu.make_async_remote_copy(
            parts.at[pl.ds(16 * (1 - core), 16)], halves,
            sum_send.at[level, 0], sum_recv.at[level, 0], twin, MESH,
        )

    def sum_halves(level):
        halves_copy(level).start()

    def sum_scatter(level):
        parts, halves, folded, gathered = buffers_of(level)[:4]
        halves_copy(level).wait()
        mine = parts[pl.ds(16 * core, 16)].astype(F32)
        folded[...] = (mine + halves[...].astype(F32)).astype(BF16)

        @pl.loop(1, 16)
        def _(step):
            other, device = plane_peer(step)
            pltpu.make_async_remote_copy(
                folded.at[other], gathered.at[place],
                sum_send.at[level, 1], sum_recv.at[level, 1], device, MESH,
            ).start()

        gathered[place] = folded[place]

    def sum_across(level):
        _, _, folded, gathered, own, across, _ = buffers_of(level)
        bulk_wait(folded, 15, sum_send.at[level, 1])
        bulk_wait(gathered, 15, sum_recv.at[level, 1])
        own[0] = jnp.sum(gathered[...].astype(F32), axis=0).astype(BF16)

        @pl.loop(1, 8)
        def _(step):
            _, device = depth_peer(step)
            pltpu.make_async_remote_copy(
                own.at[0], across.at[depth_index],
                sum_send.at[level, 2], sum_recv.at[level, 2], device, MESH,
            ).start()

        across[depth_index] = own[0]

    def sum_spread(level):
        across, total = buffers_of(level)[5:]
        bulk_wait(across, 7, sum_send.at[level, 2])
        bulk_wait(across, 7, sum_recv.at[level, 2])
        total[plane_index] = jnp.sum(across[...].astype(F32), axis=0).astype(BF16)

        @pl.loop(1, 16)
        def _(step):
            _, device = plane_peer(step)
            pltpu.make_async_remote_copy(
                total.at[plane_index], total.at[plane_index],
                sum_send.at[level, 3], sum_recv.at[level, 3], device, MESH,
            ).start()

    def share_copy(level):
        half = buffers_of(level)[6].at[pl.ds(16 * core, 16)]
        return pltpu.make_async_remote_copy(
            half, half, sum_send.at[level, 4], sum_recv.at[level, 4], twin, MESH
        )

    def sum_share(level):
        total = buffers_of(level)[6]
        bulk_wait(total, 15, sum_send.at[level, 3])
        bulk_wait(total, 15, sum_recv.at[level, 3])
        share_copy(level).start()

    def sum_finish(level):
        total = buffers_of(level)[6]
        share_copy(level).wait()
        if level in (0, 4):
            sums_small_ref[level // 4] = total[...].reshape(512, 128)
        else:
            sums_mid_ref[level - 1] = total[...].reshape(1024, 128)

    def weight_part(level):
        parts = buffers_of(level)[0]
        delta = deltas[level, 8:16].astype(F32).reshape(512, 128)
        row = lax.broadcasted_iota(jnp.int32, (512, 128), 0) % 64
        delta = jnp.where((row >= 8) & (row < 48), delta, 0.0)
        moved = jnp.concatenate(
            [pltpu.roll(delta, 511, 0), delta, pltpu.roll(delta, 1, 0)], axis=1
        ).astype(BF16)
        inputs = three_planes(acts.at[level], 8, 8)
        if level == 0:
            raw = dot(inputs, moved, TN)
        else:
            raw = dot(moved, inputs, TN)
        count = 24 if level in (0, 4) else 64
        lane = lax.broadcasted_iota(jnp.int32, (count, 128), 1)
        slots, lower, turned = [], [], []
        for a in range(3):
            for b in range(3):
                first = raw[a * 128 : a * 128 + count, b * 128 : b * 128 + 128]
                second = raw[a * 128 + 64 : a * 128 + 64 + count, b * 128 : b * 128 + 128]
                roll = pltpu.roll(second, 64, 1)
                slots.append(first + jnp.where(lane < 64, roll, 0.0))
                lower.append(second)
                turned.append(roll)
        for k in range(5):
            left = lower[2 * k + 1] if k < 4 else jnp.zeros((count, 128), F32)
            slots.append(jnp.where(lane < 64, left, turned[2 * k]))
        if count == 64:
            for k in range(14):
                parts[2 * k : 2 * k + 2] = slots[k].astype(BF16).reshape(2, 32, 128)
        else:
            for k in range(7):
                both = jnp.concatenate([slots[2 * k], slots[2 * k + 1]], axis=0)
                parts[3 * k : 3 * k + 3] = both.astype(BF16).reshape(3, 16, 128)

    blocks_wait(stage_delta, deltas.at[4], 1)
    for level in (4, 3, 2, 1, 0):
        weight_part(level)
        sum_halves(level)
        taps = taps_ref[level]
        if level == 0:
            wide = jnp.concatenate(
                [jnp.concatenate([taps[3 * k + j] for k in (2, 1, 0)], axis=1) for j in range(3)],
                axis=0,
            )
        else:
            wide = jnp.concatenate(
                [jnp.concatenate([taps[3 * k + j] for j in range(3)], axis=1) for k in (2, 1, 0)],
                axis=0,
            )
        for first, count in ranges(8 - level, 16 + level):
            out = dot(three_planes(deltas.at[level], first, count), wide, NT if level == 0 else NN)
            rows = count * 64
            back = (
                pltpu.roll(out[:, :128], rows - 1, 0)
                + out[:, 128:256]
                + pltpu.roll(out[:, 256:], 1, 0)
            ).reshape(count, 64, 128)
            if level > 0:
                slope = slopes[level - 1, first : first + count]
                deltas[level - 1, first : first + count] = (back * slope).astype(BF16)
            else:
                back_core[first - 8 : first - 8 + count] = back[:, 8:48]
        sum_scatter(level)
        if level == 0:
            sum_across(4)

    @pl.loop(1, 8)
    def _(turn):
        other = lax.rem(y_block + turn, 8)
        pltpu.make_async_remote_copy(
            back_core.at[other], back_rows.at[y_block],
            block_send.at[2, 0], block_recv.at[2, 0], (subj, z_block * 8 + other), MESH,
        ).start()

    back_rows[y_block] = back_core[y_block]
    sum_across(3)
    sum_across(2)
    sum_across(1)
    sum_spread(4)
    sum_across(0)
    for level in (3, 2, 1, 0):
        sum_spread(level)
    bulk_wait(back_core, 7, block_send.at[2, 0])
    bulk_wait(back_rows, 7, block_recv.at[2, 0])
    grad_ref[...] = direct[...] + back_rows[...].reshape(NY, 128)
    for level in (4, 3, 2, 1, 0):
        sum_share(level)
    for level in (4, 3, 2, 1, 0):
        sum_finish(level)


def main_call(u, s, up, image, weights, kt):
    eu, es, eo, rows, rows_back, depth, depth_back, spread = tables()
    vmem = pl.BlockSpec(memory_space=pltpu.VMEM)
    hbm = pl.BlockSpec(memory_space=pl.ANY)
    big = [rows, rows_back, depth, depth_back, spread]
    return pl.pallas_call(
        main_kernel,
        out_shape=(
            jax.ShapeDtypeStruct((NY, 128), F32),
            jax.ShapeDtypeStruct((3, 1024, 128), BF16),
            jax.ShapeDtypeStruct((2, 512, 128), BF16),
        ),
        in_specs=[vmem] * 13 + [hbm] * 5,
        out_specs=(vmem, vmem, vmem),
        scratch_shapes=[pltpu.VMEM(t.shape, BF16) for t in big]
        + [
            pltpu.VMEM((5, 9, 128, 128), BF16),
            pltpu.VMEM((256, 768), BF16),
            pltpu.VMEM((NY, 512), F32),
            pltpu.VMEM((SLABS, 16, 128), BF16),
            pltpu.VMEM((SLABS, 16, 128), BF16),
            pltpu.VMEM((896, 128), BF16),
            pltpu.VMEM((SLABS, 16, 128), BF16),
            pltpu.VMEM((SLABS, 16, 128), BF16),
            pltpu.VMEM((1024, 256), BF16),
            pltpu.VMEM((19, 448, 128), F32),
            pltpu.VMEM((NY, 128), F32),
            pltpu.VMEM((NY + 24, 128), F32),
            pltpu.VMEM((8, 64, 128), BF16),
            pltpu.VMEM((8, 64, 128), BF16),
            pltpu.VMEM((5, 24, 64, 128), BF16),
            pltpu.VMEM((4, 24, 64, 128), F32),
            pltpu.VMEM((5, 24, 64, 128), BF16),
            pltpu.VMEM((24, 64, 128), F32),
            pltpu.VMEM((8, 40, 128), F32),
            pltpu.VMEM((8, 40, 128), F32),
            pltpu.VMEM((3, 32, 32, 128), BF16),
            pltpu.VMEM((2, 32, 16, 128), BF16),
        ]
        + [
            pltpu.VMEM(shape, BF16)
            for _ in range(3)
            for shape in ((3, 16, 32, 128), (2, 16, 16, 128))
        ]
        + [
            pltpu.VMEM((3, 1, 32, 128), BF16),
            pltpu.VMEM((2, 1, 16, 128), BF16),
            pltpu.VMEM((3, 8, 32, 128), BF16),
            pltpu.VMEM((2, 8, 16, 128), BF16),
            pltpu.VMEM((3, 32, 32, 128), BF16),
            pltpu.VMEM((2, 32, 16, 128), BF16),
            pltpu.SemaphoreType.DMA((5,)),
            pltpu.SemaphoreType.DMA((2,)),
            pltpu.SemaphoreType.DMA((2,)),
            pltpu.SemaphoreType.DMA((3, 3)),
            pltpu.SemaphoreType.DMA((3, 3)),
            pltpu.SemaphoreType.DMA((5, 5)),
            pltpu.SemaphoreType.DMA((5, 5)),
        ],
        compiler_params=pltpu.CompilerParams(
            collective_id=0, has_side_effects=True, vmem_limit_bytes=50 * 1024 * 1024
        ),
        cost_estimate=pl.CostEstimate(
            flops=8_000_000_000, bytes_accessed=20_000_000, transcendentals=400_000
        ),
        name="step",
    )(u, s, up, image, *weights, kt, eu, es, eo, rows, rows_back, depth, depth_back, spread)


def finish_kernel(scale, mid_ref, small_ref, first_ref, second_ref, third_ref, fourth_ref, last_ref):
    def place(source, count, keep, target, tap_of):
        def rows_at(slot):
            if count == 64:
                return source[slot * 64 : slot * 64 + 64, :].astype(F32)
            start = (slot // 2) * 48
            both = source[start : start + 48, :].astype(F32)
            return both[(slot % 2) * 24 : (slot % 2) * 24 + 24]

        def left(block):
            return block[:keep, :64] * scale

        def right(block):
            return pltpu.roll(block, 64, 1)[:keep, :64] * scale

        for a in range(3):
            for b in range(3):
                block = rows_at(a * 3 + b)
                target[tap_of(a, b, 0)] = left(block)
                target[tap_of(a, b, 1)] = right(block)
        for k in range(5):
            block = rows_at(9 + k)
            target[tap_of((2 * k) // 3, (2 * k) % 3, 2)] = right(block)
            if k < 4:
                target[tap_of((2 * k + 1) // 3, (2 * k + 1) % 3, 2)] = left(block)

    def usual(a, b, kind):
        return b * 9 + (1, 2, 0)[kind] * 3 + a

    def turned(a, b, kind):
        return a * 9 + (1, 0, 2)[kind] * 3 + b

    place(small_ref.at[0], 24, 20, first_ref, turned)
    place(mid_ref.at[0], 64, 64, second_ref, usual)
    place(mid_ref.at[1], 64, 64, third_ref, usual)
    place(mid_ref.at[2], 64, 64, fourth_ref, usual)
    place(small_ref.at[1], 24, 20, last_ref, usual)


def finish_call(mid, small, cells):
    shapes = [(27, 20, 64), (27, 64, 64), (27, 64, 64), (27, 64, 64), (27, 20, 64)]
    return pl.pallas_call(
        functools.partial(finish_kernel, 1.0 / math.sqrt(cells)),
        out_shape=[jax.ShapeDtypeStruct(shape, F32) for shape in shapes],
        in_specs=[pl.BlockSpec(memory_space=pltpu.VMEM)] * 2,
        out_specs=[pl.BlockSpec(memory_space=pltpu.VMEM)] * 5,
        compiler_params=pltpu.CompilerParams(vmem_limit_bytes=24 * 1024 * 1024),
        name="finish",
    )(mid, small)


def body(image, upstream, coil_maps, kernel, w_first, w_second, w_third, w_fourth, w_last):
    u = upstream[0].reshape(40, NY).astype(BF16)
    s = coil_maps[0].reshape(32, NY).astype(BF16)

    def cells_first(block):
        turned = jnp.transpose(block, (2, 1, 0))
        return jnp.pad(turned, ((0, 0), (0, 0), (0, 44))).reshape(NY, 128)

    up = cells_first(upstream[0, :, 0])
    image_cells = cells_first(image[0, :, 0])
    weights = (
        jnp.swapaxes(w_first.reshape(27, 64, 20), 1, 2),
        w_second.reshape(27, 64, 64),
        w_third.reshape(27, 64, 64),
        w_fourth.reshape(27, 64, 64),
        w_last.reshape(27, 20, 64),
    )
    kt = jnp.transpose(kernel, (4, 3, 2, 0, 1)).astype(BF16).reshape(10, NZ, 100)
    kt = jnp.pad(kt, ((0, 0), (0, 0), (0, 28)))
    grad, mid, small = main_call(u, s, up, image_cells, weights, kt)
    cells = (
        lax.axis_size("subj") * image.shape[0] * lax.axis_size("slab") * image.shape[2] * 2 * NY
    )
    first, second, third, fourth, last = finish_call(mid, small, cells)
    image_grad = jnp.transpose(grad.reshape(NY, 2, 64)[:, :, :20], (2, 1, 0))[None, :, None]
    return (
        image_grad,
        jnp.swapaxes(first, 1, 2).reshape(3, 3, 3, 64, 20),
        second.reshape(3, 3, 3, 64, 64),
        third.reshape(3, 3, 3, 64, 64),
        fourth.reshape(3, 3, 3, 64, 64),
        last.reshape(3, 3, 3, 20, 64),
    )


def solution(mesh):
    in_specs = (
        P("subj", None, "slab", None, None),
        P("subj", None, "slab", None, None),
        P("subj", None, None, "slab", None, None),
        P(None, None, None, None, "slab"),
        P(),
        P(),
        P(),
        P(),
        P(),
    )
    out_specs = (P("subj", None, "slab", None, None), P(), P(), P(), P(), P())
    return jax.shard_map(body, mesh=mesh, in_specs=in_specs, out_specs=out_specs, check_vma=False)
```

```python
import functools
import math

import jax
import jax.numpy as jnp
import ml_dtypes
import numpy as np
from jax import lax
from jax.experimental import pallas as pl
from jax.experimental.pallas import tpu as pltpu
from jax.sharding import PartitionSpec as P

F32 = jnp.float32
BF16 = jnp.bfloat16
MESH = pl.DeviceIdType.MESH
NN = (((1,), (0,)), ((), ()))
NT = (((1,), (1,)), ((), ()))
TN = (((0,), (0,)), ((), ()))
SLABS = 64
NY = 320
NZ = 64
STEP = 8


def lane_of(x, comp, coil):
    group = x * 2 + coil // 4
    base = group * 40 if group < 3 else 128
    return base + comp * 4 + coil % 4


def slot_block(q, j):
    if q < 5:
        return q, j // 2
    if q == 5:
        return j, 1
    return min(3 + j, 4), 1


@functools.lru_cache(None)
def tables():
    half = ml_dtypes.bfloat16
    expand_u = np.zeros((2, 512, 20), np.float32)
    expand_s = np.zeros((2, 512, 16), np.float32)
    collect = np.zeros((512, 128), np.float32)
    for x in range(2):
        for comp in range(10):
            for coil in range(8):
                lane = lane_of(x, comp, coil)
                for part in range(2):
                    expand_u[x, part * 256 + lane, part * 10 + comp] = 1
                    expand_s[x, part * 256 + lane, part * 8 + coil] = 1
                    collect[part * 256 + lane, x * 64 + part * 10 + comp] = 1
    y = np.arange(NY)
    angle = 2 * np.pi * ((y[:, None] * y[None, :]) % NY) / NY
    cos = (np.cos(angle) / math.sqrt(NY)).reshape(SLABS, 5, NY)
    sin = (np.sin(angle) / math.sqrt(NY)).reshape(SLABS, 5, NY)
    rows = np.zeros((SLABS, 16, 2, 384), np.float32)
    rows[:, 0:10:2, 0, :NY] = cos
    rows[:, 0:10:2, 1, :NY] = sin
    rows[:, 1:10:2, 0, :NY] = -sin
    rows[:, 1:10:2, 1, :NY] = cos
    rows = rows.reshape(1024, 768)
    rows_back = np.zeros((2, NY, SLABS, 16), np.float32)
    cos_t, sin_t = np.moveaxis(cos, 2, 0), np.moveaxis(sin, 2, 0)
    rows_back[0, :, :, 0:10:2] = cos_t
    rows_back[0, :, :, 1:10:2] = -sin_t
    rows_back[1, :, :, 0:10:2] = sin_t
    rows_back[1, :, :, 1:10:2] = cos_t
    rows_back = rows_back.reshape(640, 1024)
    z = np.arange(NZ)
    angle = 2 * np.pi * ((z[:, None] * z[None, :]) % NZ) / NZ
    cos, sin = np.cos(angle) / 8, np.sin(angle) / 8
    depth = np.zeros((7, 2, NZ, NZ, 16), np.float32)
    depth_back = np.zeros((NZ, 16, 7, 2, NZ), np.float32)
    for q in range(7):
        depth[q, 0, :, :, 2 * q] = cos
        depth[q, 0, :, :, 2 * q + 1] = sin
        depth[q, 1, :, :, 2 * q] = -sin
        depth[q, 1, :, :, 2 * q + 1] = cos
        depth_back[:, 2 * q, q, 0] = cos
        depth_back[:, 2 * q, q, 1] = -sin
        depth_back[:, 2 * q + 1, q, 0] = sin
        depth_back[:, 2 * q + 1, q, 1] = cos
    depth = depth.reshape(896, 1024)
    depth_back = depth_back.reshape(1024, 896)
    spread = np.zeros((384, 20, 128), np.float32)
    for shift in range(-9, 10):
        for j in range(3):
            for comp in range(10):
                other = comp + shift
                if 0 <= other < 10:
                    first = j * 40 + comp * 4
                    spread[j * 128 + comp * 10 + other, shift + 9, first : first + 4] = 1
    spread = spread.reshape(384, 2560)
    out = (expand_u, expand_s, collect, rows, rows_back, depth, depth_back, spread)
    return tuple(t.astype(half) for t in out)


def dot(a, b, dims=NN):
    return lax.dot_general(a, b, dims, preferred_element_type=F32)


def main_kernel(*refs):
    sources, refs = refs[:17], refs[17:]
    grad_ref, sums_mid_ref, sums_small_ref = refs[:3]
    held, refs = refs[3:20], refs[20:]
    (
        up_ref, s_ref, eu_ref, es_ref, rows_t, image_ref, w1_ref, w2_ref, w3_ref, w4_ref, w5_ref,
        k_ref, spread_t, depth_t, depth_back_t, eo_ref, rows_back_t,
    ) = held
    (
        taps_ref, coil, maps, message, arrived, mixed, message_back, returned, unpacked, coefs,
        direct, up_rows, padded, stage_image, stage_delta, packed_image, packed_delta, acts, slopes,
        deltas, inside, back_core, back_rows, parts_mid, parts_small, halves_mid, halves_small,
        folded_mid, folded_small, gathered_mid, gathered_small, own_mid, own_small, across_mid,
        across_small, total_mid, total_small, table_sem, send_sem, recv_sem, block_send, block_recv,
        sum_send, sum_recv,
    ) = refs
    subj = lax.axis_index("subj")
    slab = lax.axis_index("slab")
    z_hi, core = subj // 2, subj % 2
    z_lo, place = slab // 16, slab % 16
    plane_index = core * 16 + place
    depth_index = z_hi * 4 + z_lo

    def slab_peer(step):
        return (subj, lax.rem(slab + step, SLABS))

    def plane_peer(step):
        other = lax.rem(place + step, 16)
        return other, (subj, z_lo * 16 + other)

    twin = (z_hi * 2 + 1 - core, slab)

    def depth_peer(step):
        other = lax.rem(depth_index + step, 8)
        return other, ((other // 4) * 2 + core, (other % 4) * 16 + place)

    z_block, y_block = slab // 8, slab % 8
    zero_planes = jnp.zeros((8, 32, 128), BF16)
    for first, edge in ((0, 0), (16, 7)):

        @pl.when(z_block == edge)
        def _(first=first):
            packed_image[first : first + 8] = zero_planes
            packed_delta[first : first + 8] = zero_planes

    barrier = pltpu.get_barrier_semaphore()

    def greet(device):
        pl.semaphore_signal(barrier, inc=1, device_id=device, device_id_type=MESH)

    @pl.loop(1, SLABS)
    def _(step):
        greet(slab_peer(step))

    greet(twin)

    @pl.loop(0, 4)
    def _(other):
        greet(((1 - z_hi) * 2 + core, other * 16 + place))

    fetches = [
        pltpu.make_async_copy(source, target, table_sem.at[i])
        for i, (source, target) in enumerate(zip(sources, held))
    ]
    for fetch in fetches[:12]:
        fetch.start()

    for i in range(3):
        parts_mid[i, 28:32] = jnp.zeros((4, 32, 128), BF16)
    for i in range(2):
        parts_small[i, 21:32] = jnp.zeros((11, 16, 128), BF16)
    def cut(block, stage):
        padded[8 : 8 + NY, :] = block
        for piece in range(8):
            upper = padded[40 * piece : 40 * piece + 32, :]
            lower = padded[40 * piece + 32 : 40 * piece + 64, :]
            stage[piece] = (upper + pltpu.roll(lower, 32, 1)).astype(BF16)

    def unpack(source, target):
        block = source[...]
        lower = pltpu.roll(block.astype(F32).reshape(24 * 32, 128), 96, 1).astype(BF16)
        target[:, 0:32] = block
        target[:, 32:64] = lower.reshape(24, 32, 128)

    padded[0:8, :] = jnp.zeros((8, 128), F32)
    padded[8 + NY :, :] = jnp.zeros((16, 128), F32)

    def blocks_send(stage, target, which):
        for group, step in ((1, -1), (2, 1), (0, 0)):
            other_block = jnp.clip(z_block + step, 0, 7)
            slot = y_block + 8 - 8 * step

            @pl.when(z_block + step == other_block)
            def _():
                @pl.loop(0 if step else 1, 8)
                def _(turn):
                    piece = lax.rem(y_block + turn, 8)
                    pltpu.make_async_remote_copy(
                        stage.at[piece], target.at[slot],
                        block_send.at[which, group], block_recv.at[which, group],
                        (subj, other_block * 8 + piece), MESH,
                    ).start()

        target[y_block + 8] = stage[y_block]

    def blocks_wait(stage, target, which):
        bulk_wait(stage, 7, block_send.at[which, 0])
        bulk_wait(target, 7, block_recv.at[which, 0])

        @pl.when(z_block > 0)
        def _():
            bulk_wait(stage, 8, block_send.at[which, 1])
            bulk_wait(target, 8, block_recv.at[which, 2])

        @pl.when(z_block < 7)
        def _():
            bulk_wait(stage, 8, block_send.at[which, 2])
            bulk_wait(target, 8, block_recv.at[which, 1])

    def exchange_start(source, target, which):
        @pl.loop(1, SLABS)
        def _(step):
            subject, other = slab_peer(step)
            pltpu.make_async_remote_copy(
                source.at[other], target.at[slab], send_sem.at[which], recv_sem.at[which],
                (subject, other), MESH,
            ).start()

        target[slab] = source[slab]

    def bulk_wait(buffer, count, semaphore):
        piece = buffer.at[pl.ds(0, count)]
        pltpu.make_async_copy(piece, piece, semaphore).wait()

    def exchange_wait(source, target, which):
        bulk_wait(source, SLABS - 1, send_sem.at[which])
        bulk_wait(target, SLABS - 1, recv_sem.at[which])

    for fetch in fetches[:4]:
        fetch.wait()
    lane = lax.broadcasted_iota(jnp.int32, (20, 128), 1)
    channel = lax.broadcasted_iota(jnp.int32, (20, 128), 0)
    places = [jnp.where(lane == x * 64 + channel, 1.0, 0.0).astype(BF16) for x in range(2)]
    u_high = [up_ref[:, x, :].astype(BF16) for x in range(2)]
    s_high = [s_ref[:, x, :].astype(BF16) for x in range(2)]
    wide_u = dot(eu_ref[0], u_high[0]) + dot(eu_ref[1], u_high[1])
    wide_s = dot(es_ref[0], s_high[0]) + dot(es_ref[1], s_high[1])
    u_re, u_im = wide_u[:256], wide_u[256:]
    s_re, s_im = wide_s[:256], wide_s[256:]
    coil[...] = jnp.zeros((256, 768), BF16)
    coil[:, 0:NY] = (s_re * u_re - s_im * u_im).astype(BF16)
    coil[:, 384 : 384 + NY] = (s_re * u_im + s_im * u_re).astype(BF16)
    fetches[4].wait()
    sub = lax.broadcasted_iota(jnp.int32, (8, 8, 128), 1) // 2

    @pl.loop(0, 8)
    def _(step):
        first = pl.multiple_of(step * 128, 128)
        spectra = dot(rows_t[pl.ds(first, 128), :], coil[...], NT)
        body = spectra[:, :128].reshape(8, 2, 8, 128)
        rest = spectra[:, 128:].reshape(8, 2, 8, 128)
        low, high = rest[:, 0], rest[:, 1]
        lowered = pltpu.roll(low, 6, 1)
        at_one = pltpu.roll(low, 2, 1) + pltpu.roll(low, 40, 2) + pltpu.roll(lowered, 80, 2)
        at_two = lowered + pltpu.roll(pltpu.roll(high, 4, 1), 40, 2)
        extra = jnp.where(sub == 1, at_one, jnp.where(sub == 2, at_two, 0.0))
        packed = jnp.concatenate([body[:, 0:1], (body[:, 1] + extra)[:, None]], axis=1)
        message[pl.ds(step * 8, 8)] = packed.reshape(8, 16, 128).astype(BF16)

    slot_z = lax.broadcasted_iota(jnp.int32, (24, 64, 128), 0) + (z_block * 8 - 8)
    slot_y = lax.broadcasted_iota(jnp.int32, (24, 64, 128), 1) + (y_block * 40 - 8)
    grid_ok = (slot_z >= 0) & (slot_z < NZ) & (slot_y >= 0) & (slot_y < NY)
    inside[...] = jnp.where(grid_ok, 1.0, 0.0)

    def three_planes(buffer, first, count):
        pieces = [buffer[first + k : first + k + count].reshape(count * 64, 128) for k in (-1, 0, 1)]
        return jnp.concatenate(pieces, axis=1)

    def ranges(low, high):
        return [(first, min(STEP, high - first)) for first in range(low, high, STEP)]

    def forward(level):
        taps = taps_ref[level]
        if level == 0:
            wide = jnp.concatenate(
                [jnp.concatenate([taps[3 * k + j] for j in range(3)], axis=1) for k in range(3)],
                axis=0,
            )
        else:
            wide = jnp.concatenate(
                [taps[3 * k : 3 * k + 3].reshape(384, 128) for k in range(3)], axis=1
            )
        for first, count in ranges(level + 1, 23 - level):
            out = dot(three_planes(acts.at[level], first, count), wide, NN if level == 0 else NT)
            rows = count * 64
            pre = (
                pltpu.roll(out[:, :128], 1, 0)
                + out[:, 128:256]
                + pltpu.roll(out[:, 256:], rows - 1, 0)
            )
            keep = inside[first : first + count].reshape(rows, 128)
            sigmoid = jax.nn.sigmoid(pre) * keep
            value = pre * sigmoid
            slope = sigmoid + value * (1.0 - jax.nn.sigmoid(pre))
            acts[level + 1, first : first + count] = value.astype(BF16).reshape(count, 64, 128)
            slopes[level, first : first + count] = slope.reshape(count, 64, 128)

    for fetch in fetches[12:]:
        fetch.start()
    fetches[5].wait()
    image = image_ref[...].astype(F32)
    cut(
        sum(dot(image[:, x, :].astype(BF16), places[x], TN) for x in range(2)), stage_image
    )
    crossed = (((0,), (1,)), ((), ()))
    maps[...] = dot(s_high[0], es_ref[0], crossed) + dot(s_high[1], es_ref[1], crossed)
    rows_sum = jnp.zeros((NY, 128), F32)
    for x in range(2):
        low = (up_ref[:, x, :] - u_high[x].astype(F32)).astype(BF16)
        rows_sum += dot(u_high[x], places[x], TN) + dot(low, places[x], TN)
    up_rows[...] = rows_sum
    for fetch in fetches[6:12]:
        fetch.wait()
    for level, w_ref in enumerate((w1_ref, w2_ref, w3_ref, w4_ref, w5_ref)):
        for tap in range(9):
            low, middle, high = [
                w_ref[(tap // 3) * 9 + off_x * 3 + tap % 3].astype(F32) for off_x in range(3)
            ]
            if level == 0:
                low, high = high, low
            pieces = [jnp.concatenate(pair, axis=1) for pair in ((middle, high), (low, middle))]
            if level in (0, 4):
                pieces = [
                    jnp.concatenate([piece, jnp.zeros((44, 128), F32)], axis=0) for piece in pieces
                ]
            taps_ref[level, tap] = jnp.concatenate(pieces, axis=0).astype(BF16)

    pl.semaphore_wait(barrier, 68)
    exchange_start(message, arrived, 0)
    blocks_send(stage_image, packed_image, 0)
    fetches[12].wait()
    columns = []
    for q in range(7):
        rows = []
        for j in range(3):
            ky, x = slot_block(q, j)
            rows += [k_ref[:, ky, x, :], jnp.zeros((28, NZ), F32)]
        columns.append(jnp.concatenate(rows, axis=0))
    stacked = jnp.concatenate(columns, axis=1).astype(BF16)
    for step in range(10):
        pair = dot(stacked, spread_t[:, step * 256 : step * 256 + 256], TN)
        coefs[2 * step] = pair[:, :128]
        if step < 9:
            coefs[2 * step + 1] = pair[:, 128:]

    fetches[13].wait()
    fetches[14].wait()
    exchange_wait(message, arrived, 0)

    for q in range(7):
        first = q * 128
        spectrum = dot(depth_t[pl.ds(first, 128), :], arrived[...].reshape(1024, 128))
        real, imag = spectrum[:64], spectrum[64:]
        out_real = jnp.zeros((64, 128), F32)
        out_imag = jnp.zeros((64, 128), F32)
        for shift in range(-9, 10):
            factor = coefs[shift + 9, q * 64 : q * 64 + 64, :]
            turn = (-4 * shift) % 128
            moved_real = real if turn == 0 else pltpu.roll(real, turn, 1)
            moved_imag = imag if turn == 0 else pltpu.roll(imag, turn, 1)
            out_real += factor * moved_real
            out_imag += factor * moved_imag
        mixed[pl.ds(first, 64), :] = out_real.astype(BF16)
        mixed[pl.ds(first + 64, 64), :] = out_imag.astype(BF16)

    for step in range(2):
        first = step * 512
        back = dot(depth_back_t[pl.ds(first, 512), :], mixed[...])
        message_back[pl.ds(step * 32, 32)] = back.astype(BF16).reshape(32, 16, 128)

    exchange_start(message_back, returned, 1)
    blocks_wait(stage_image, packed_image, 0)
    unpack(packed_image, acts.at[0])
    for level in range(4):
        forward(level)
    exchange_wait(message_back, returned, 1)

    @pl.loop(0, 8)
    def _(step):
        block = returned[pl.ds(step * 8, 8)].astype(F32)
        body = block.reshape(8, 2, 8, 128)[:, 1]
        raised = pltpu.roll(body, 2, 1)
        low = jnp.where(
            sub == 0,
            pltpu.roll(body, 6, 1),
            jnp.where(
                sub == 1,
                pltpu.roll(body, 88, 2),
                jnp.where(sub == 2, pltpu.roll(raised, 48, 2), raised),
            ),
        )
        high = jnp.where(sub == 0, pltpu.roll(pltpu.roll(body, 4, 1), 88, 2), 0.0)
        rest = jnp.concatenate([low[:, None], high[:, None]], axis=1).reshape(128, 128)
        first = pl.multiple_of(step * 128, 128)
        unpacked[pl.ds(first, 128), 0:128] = block.reshape(128, 128).astype(BF16)
        unpacked[pl.ds(first, 128), 128:256] = rest.astype(BF16)

    fetches[15].wait()
    fetches[16].wait()
    back_re = dot(rows_back_t[0:NY, :], unpacked[...])
    back_im = dot(rows_back_t[NY:, :], unpacked[...])
    s_re, s_im = maps[:, :256], maps[:, 256:]
    out_re = (s_re * back_re + s_im * back_im).astype(BF16)
    out_im = (s_re * back_im - s_im * back_re).astype(BF16)
    normal = dot(out_re, eo_ref[0:256, :]) + dot(out_im, eo_ref[256:, :])
    own_direct = up_rows[...] - 0.5 * normal
    direct[...] = own_direct
    cut(own_direct, stage_delta)
    blocks_send(stage_delta, packed_delta, 1)

    def buffers_of(level):
        if level in (0, 4):
            every = (
                parts_small, halves_small, folded_small, gathered_small, own_small,
                across_small, total_small,
            )
            return [buffer.at[level // 4] for buffer in every]
        every = (
            parts_mid, halves_mid, folded_mid, gathered_mid, own_mid, across_mid, total_mid,
        )
        return [buffer.at[level - 1] for buffer in every]

    def halves_copy(level):
        parts, halves = buffers_of(level)[:2]
        return pltpu.make_async_remote_copy(
            parts.at[pl.ds(16 * (1 - core), 16)], halves,
            sum_send.at[level, 0], sum_recv.at[level, 0], twin, MESH,
        )

    def sum_halves(level):
        halves_copy(level).start()

    def sum_scatter(level):
        parts, halves, folded, gathered = buffers_of(level)[:4]
        halves_copy(level).wait()
        mine = parts[pl.ds(16 * core, 16)].astype(F32)
        folded[...] = (mine + halves[...].astype(F32)).astype(BF16)

        @pl.loop(1, 16)
        def _(step):
            other, device = plane_peer(step)
            pltpu.make_async_remote_copy(
                folded.at[other], gathered.at[place],
                sum_send.at[level, 1], sum_recv.at[level, 1], device, MESH,
            ).start()

        gathered[place] = folded[place]

    def sum_across(level):
        _, _, folded, gathered, own, across, _ = buffers_of(level)
        bulk_wait(folded, 15, sum_send.at[level, 1])
        bulk_wait(gathered, 15, sum_recv.at[level, 1])
        own[0] = jnp.sum(gathered[...].astype(F32), axis=0).astype(BF16)

        @pl.loop(1, 8)
        def _(step):
            _, device = depth_peer(step)
            pltpu.make_async_remote_copy(
                own.at[0], across.at[depth_index],
                sum_send.at[level, 2], sum_recv.at[level, 2], device, MESH,
            ).start()

        across[depth_index] = own[0]

    def sum_spread(level):
        across, total = buffers_of(level)[5:]
        bulk_wait(across, 7, sum_send.at[level, 2])
        bulk_wait(across, 7, sum_recv.at[level, 2])
        total[plane_index] = jnp.sum(across[...].astype(F32), axis=0).astype(BF16)

        @pl.loop(1, 16)
        def _(step):
            _, device = plane_peer(step)
            pltpu.make_async_remote_copy(
                total.at[plane_index], total.at[plane_index],
                sum_send.at[level, 3], sum_recv.at[level, 3], device, MESH,
            ).start()

    def share_copy(level):
        half = buffers_of(level)[6].at[pl.ds(16 * core, 16)]
        return pltpu.make_async_remote_copy(
            half, half, sum_send.at[level, 4], sum_recv.at[level, 4], twin, MESH
        )

    def sum_share(level):
        total = buffers_of(level)[6]
        bulk_wait(total, 15, sum_send.at[level, 3])
        bulk_wait(total, 15, sum_recv.at[level, 3])
        share_copy(level).start()

    def sum_finish(level):
        total = buffers_of(level)[6]
        share_copy(level).wait()
        if level in (0, 4):
            sums_small_ref[level // 4] = total[...].reshape(512, 128)
        else:
            sums_mid_ref[level - 1] = total[...].reshape(1024, 128)

    def weight_part(level):
        parts = buffers_of(level)[0]
        delta = deltas[level, 8:16].astype(F32).reshape(512, 128)
        row = lax.broadcasted_iota(jnp.int32, (512, 128), 0) % 64
        delta = jnp.where((row >= 8) & (row < 48), delta, 0.0)
        moved = jnp.concatenate(
            [pltpu.roll(delta, 511, 0), delta, pltpu.roll(delta, 1, 0)], axis=1
        ).astype(BF16)
        inputs = three_planes(acts.at[level], 8, 8)
        if level == 0:
            raw = dot(inputs, moved, TN)
        else:
            raw = dot(moved, inputs, TN)
        count = 24 if level in (0, 4) else 64
        lane = lax.broadcasted_iota(jnp.int32, (count, 128), 1)
        slots, lower, turned = [], [], []
        for a in range(3):
            for b in range(3):
                first = raw[a * 128 : a * 128 + count, b * 128 : b * 128 + 128]
                second = raw[a * 128 + 64 : a * 128 + 64 + count, b * 128 : b * 128 + 128]
                roll = pltpu.roll(second, 64, 1)
                slots.append(first + jnp.where(lane < 64, roll, 0.0))
                lower.append(second)
                turned.append(roll)
        for k in range(5):
            left = lower[2 * k + 1] if k < 4 else jnp.zeros((count, 128), F32)
            slots.append(jnp.where(lane < 64, left, turned[2 * k]))
        if count == 64:
            for k in range(14):
                parts[2 * k : 2 * k + 2] = slots[k].astype(BF16).reshape(2, 32, 128)
        else:
            for k in range(7):
                both = jnp.concatenate([slots[2 * k], slots[2 * k + 1]], axis=0)
                parts[3 * k : 3 * k + 3] = both.astype(BF16).reshape(3, 16, 128)

    blocks_wait(stage_delta, packed_delta, 1)
    unpack(packed_delta, deltas.at[4])
    for level in (4, 3, 2, 1, 0):
        weight_part(level)
        sum_halves(level)
        taps = taps_ref[level]
        if level == 0:
            wide = jnp.concatenate(
                [jnp.concatenate([taps[3 * k + j] for k in (2, 1, 0)], axis=1) for j in range(3)],
                axis=0,
            )
        else:
            wide = jnp.concatenate(
                [jnp.concatenate([taps[3 * k + j] for j in range(3)], axis=1) for k in (2, 1, 0)],
                axis=0,
            )
        for first, count in ranges(8 - level, 16 + level):
            out = dot(three_planes(deltas.at[level], first, count), wide, NT if level == 0 else NN)
            rows = count * 64
            back = (
                pltpu.roll(out[:, :128], rows - 1, 0)
                + out[:, 128:256]
                + pltpu.roll(out[:, 256:], 1, 0)
            ).reshape(count, 64, 128)
            if level > 0:
                slope = slopes[level - 1, first : first + count]
                deltas[level - 1, first : first + count] = (back * slope).astype(BF16)
            else:
                back_core[first - 8 : first - 8 + count] = back[:, 8:48]
        sum_scatter(level)
        if level == 0:
            sum_across(4)

    @pl.loop(1, 8)
    def _(turn):
        other = lax.rem(y_block + turn, 8)
        pltpu.make_async_remote_copy(
            back_core.at[other], back_rows.at[y_block],
            block_send.at[2, 0], block_recv.at[2, 0], (subj, z_block * 8 + other), MESH,
        ).start()

    back_rows[y_block] = back_core[y_block]
    sum_across(3)
    sum_across(2)
    sum_across(1)
    sum_spread(4)
    sum_across(0)
    for level in (3, 2, 1, 0):
        sum_spread(level)
    bulk_wait(back_core, 7, block_send.at[2, 0])
    bulk_wait(back_rows, 7, block_recv.at[2, 0])
    grad_ref[...] = direct[...] + back_rows[...].reshape(NY, 128)
    for level in (4, 3, 2, 1, 0):
        sum_share(level)
    for level in (4, 3, 2, 1, 0):
        sum_finish(level)


def main_call(up, s, image, weights, kernel):
    eu, es, eo, rows, rows_back, depth, depth_back, spread = tables()
    vmem = pl.BlockSpec(memory_space=pltpu.VMEM)
    sources = [
        up, s, eu, es, rows, image, *weights, kernel, spread, depth, depth_back, eo, rows_back
    ]
    return pl.pallas_call(
        main_kernel,
        out_shape=(
            jax.ShapeDtypeStruct((NY, 128), F32),
            jax.ShapeDtypeStruct((3, 1024, 128), BF16),
            jax.ShapeDtypeStruct((2, 512, 128), BF16),
        ),
        in_specs=[pl.BlockSpec(memory_space=pl.ANY)] * len(sources),
        out_specs=(vmem, vmem, vmem),
        scratch_shapes=[pltpu.VMEM(t.shape, t.dtype) for t in sources]
        + [
            pltpu.VMEM((5, 9, 128, 128), BF16),
            pltpu.VMEM((256, 768), BF16),
            pltpu.VMEM((NY, 512), F32),
            pltpu.VMEM((SLABS, 16, 128), BF16),
            pltpu.VMEM((SLABS, 16, 128), BF16),
            pltpu.VMEM((896, 128), BF16),
            pltpu.VMEM((SLABS, 16, 128), BF16),
            pltpu.VMEM((SLABS, 16, 128), BF16),
            pltpu.VMEM((1024, 256), BF16),
            pltpu.VMEM((19, 448, 128), F32),
            pltpu.VMEM((NY, 128), F32),
            pltpu.VMEM((NY, 128), F32),
            pltpu.VMEM((NY + 24, 128), F32),
            pltpu.VMEM((8, 32, 128), BF16),
            pltpu.VMEM((8, 32, 128), BF16),
            pltpu.VMEM((24, 32, 128), BF16),
            pltpu.VMEM((24, 32, 128), BF16),
            pltpu.VMEM((5, 24, 64, 128), BF16),
            pltpu.VMEM((4, 24, 64, 128), F32),
            pltpu.VMEM((5, 24, 64, 128), BF16),
            pltpu.VMEM((24, 64, 128), F32),
            pltpu.VMEM((8, 40, 128), F32),
            pltpu.VMEM((8, 40, 128), F32),
            pltpu.VMEM((3, 32, 32, 128), BF16),
            pltpu.VMEM((2, 32, 16, 128), BF16),
        ]
        + [
            pltpu.VMEM(shape, BF16)
            for _ in range(3)
            for shape in ((3, 16, 32, 128), (2, 16, 16, 128))
        ]
        + [
            pltpu.VMEM((3, 1, 32, 128), BF16),
            pltpu.VMEM((2, 1, 16, 128), BF16),
            pltpu.VMEM((3, 8, 32, 128), BF16),
            pltpu.VMEM((2, 8, 16, 128), BF16),
            pltpu.VMEM((3, 32, 32, 128), BF16),
            pltpu.VMEM((2, 32, 16, 128), BF16),
            pltpu.SemaphoreType.DMA((17,)),
            pltpu.SemaphoreType.DMA((2,)),
            pltpu.SemaphoreType.DMA((2,)),
            pltpu.SemaphoreType.DMA((3, 3)),
            pltpu.SemaphoreType.DMA((3, 3)),
            pltpu.SemaphoreType.DMA((5, 5)),
            pltpu.SemaphoreType.DMA((5, 5)),
        ],
        compiler_params=pltpu.CompilerParams(
            collective_id=0, has_side_effects=True, vmem_limit_bytes=60 * 1024 * 1024
        ),
        cost_estimate=pl.CostEstimate(
            flops=8_000_000_000, bytes_accessed=20_000_000, transcendentals=400_000
        ),
        name="step",
    )(*sources)


def finish_kernel(scale, mid_ref, small_ref, first_ref, second_ref, third_ref, fourth_ref, last_ref):
    def place(source, count, keep, target, tap_of):
        def rows_at(slot):
            if count == 64:
                return source[slot * 64 : slot * 64 + 64, :].astype(F32)
            start = (slot // 2) * 48
            both = source[start : start + 48, :].astype(F32)
            return both[(slot % 2) * 24 : (slot % 2) * 24 + 24]

        def left(block):
            return block[:keep, :64] * scale

        def right(block):
            return pltpu.roll(block, 64, 1)[:keep, :64] * scale

        for a in range(3):
            for b in range(3):
                block = rows_at(a * 3 + b)
                target[tap_of(a, b, 0)] = left(block)
                target[tap_of(a, b, 1)] = right(block)
        for k in range(5):
            block = rows_at(9 + k)
            target[tap_of((2 * k) // 3, (2 * k) % 3, 2)] = right(block)
            if k < 4:
                target[tap_of((2 * k + 1) // 3, (2 * k + 1) % 3, 2)] = left(block)

    def usual(a, b, kind):
        return b * 9 + (1, 2, 0)[kind] * 3 + a

    def turned(a, b, kind):
        return a * 9 + (1, 0, 2)[kind] * 3 + b

    place(small_ref.at[0], 24, 20, first_ref, turned)
    place(mid_ref.at[0], 64, 64, second_ref, usual)
    place(mid_ref.at[1], 64, 64, third_ref, usual)
    place(mid_ref.at[2], 64, 64, fourth_ref, usual)
    place(small_ref.at[1], 24, 20, last_ref, usual)


def finish_call(mid, small, cells):
    shapes = [(27, 20, 64), (27, 64, 64), (27, 64, 64), (27, 64, 64), (27, 20, 64)]
    return pl.pallas_call(
        functools.partial(finish_kernel, 1.0 / math.sqrt(cells)),
        out_shape=[jax.ShapeDtypeStruct(shape, F32) for shape in shapes],
        in_specs=[pl.BlockSpec(memory_space=pltpu.VMEM)] * 2,
        out_specs=[pl.BlockSpec(memory_space=pltpu.VMEM)] * 5,
        compiler_params=pltpu.CompilerParams(vmem_limit_bytes=24 * 1024 * 1024),
        name="finish",
    )(mid, small)


def body(image, upstream, coil_maps, kernel, w_first, w_second, w_third, w_fourth, w_last):
    weights = (
        jnp.swapaxes(w_first.reshape(27, 64, 20), 1, 2),
        w_second.reshape(27, 64, 64),
        w_third.reshape(27, 64, 64),
        w_fourth.reshape(27, 64, 64),
        w_last.reshape(27, 20, 64),
    )
    bands = jnp.transpose(kernel, (0, 1, 4, 3, 2)).reshape(100, 5, 2, NZ)
    grad, mid, small = main_call(
        upstream[0, :, 0], coil_maps[0].reshape(16, 2, NY), image[0, :, 0], weights, bands
    )
    cells = (
        lax.axis_size("subj") * image.shape[0] * lax.axis_size("slab") * image.shape[2] * 2 * NY
    )
    first, second, third, fourth, last = finish_call(mid, small, cells)
    image_grad = jnp.transpose(grad.reshape(NY, 2, 64)[:, :, :20], (2, 1, 0))[None, :, None]
    return (
        image_grad,
        jnp.swapaxes(first, 1, 2).reshape(3, 3, 3, 64, 20),
        second.reshape(3, 3, 3, 64, 64),
        third.reshape(3, 3, 3, 64, 64),
        fourth.reshape(3, 3, 3, 64, 64),
        last.reshape(3, 3, 3, 20, 64),
    )


def solution(mesh):
    in_specs = (
        P("subj", None, "slab", None, None),
        P("subj", None, "slab", None, None),
        P("subj", None, None, "slab", None, None),
        P(None, None, None, None, "slab"),
        P(),
        P(),
        P(),
        P(),
        P(),
    )
    out_specs = (P("subj", None, "slab", None, None), P(), P(), P(), P(), P())
    return jax.shard_map(body, mesh=mesh, in_specs=in_specs, out_specs=out_specs, check_vma=False)
```

```python
import functools
import math

import jax
import jax.numpy as jnp
import ml_dtypes
import numpy as np
from jax import lax
from jax.experimental import pallas as pl
from jax.experimental.pallas import tpu as pltpu
from jax.sharding import PartitionSpec as P

F32 = jnp.float32
BF16 = jnp.bfloat16
MESH = pl.DeviceIdType.MESH
NN = (((1,), (0,)), ((), ()))
NT = (((1,), (1,)), ((), ()))
TN = (((0,), (0,)), ((), ()))
SLABS = 64
NY = 320
NZ = 64
STEP = 8


def lane_of(x, comp, coil):
    group = x * 2 + coil // 4
    base = group * 40 if group < 3 else 128
    return base + comp * 4 + coil % 4


def slot_block(q, j):
    if q < 5:
        return q, j // 2
    if q == 5:
        return j, 1
    return min(3 + j, 4), 1


@functools.lru_cache(None)
def tables():
    half = ml_dtypes.bfloat16
    expand_u = np.zeros((2, 512, 20), np.float32)
    expand_s = np.zeros((2, 512, 16), np.float32)
    collect = np.zeros((512, 128), np.float32)
    for x in range(2):
        for comp in range(10):
            for coil in range(8):
                lane = lane_of(x, comp, coil)
                for part in range(2):
                    expand_u[x, part * 256 + lane, part * 10 + comp] = 1
                    expand_s[x, part * 256 + lane, part * 8 + coil] = 1
                    collect[part * 256 + lane, x * 64 + part * 10 + comp] = 1
    y = np.arange(NY)
    angle = 2 * np.pi * ((y[:, None] * y[None, :]) % NY) / NY
    cos = (np.cos(angle) / math.sqrt(NY)).reshape(SLABS, 5, NY)
    sin = (np.sin(angle) / math.sqrt(NY)).reshape(SLABS, 5, NY)
    rows = np.zeros((SLABS, 16, 2, 384), np.float32)
    rows[:, 0:10:2, 0, :NY] = cos
    rows[:, 0:10:2, 1, :NY] = sin
    rows[:, 1:10:2, 0, :NY] = -sin
    rows[:, 1:10:2, 1, :NY] = cos
    rows = rows.reshape(1024, 768)
    rows_back = np.zeros((2, NY, SLABS, 16), np.float32)
    cos_t, sin_t = np.moveaxis(cos, 2, 0), np.moveaxis(sin, 2, 0)
    rows_back[0, :, :, 0:10:2] = cos_t
    rows_back[0, :, :, 1:10:2] = -sin_t
    rows_back[1, :, :, 0:10:2] = sin_t
    rows_back[1, :, :, 1:10:2] = cos_t
    rows_back = rows_back.reshape(640, 1024)
    z = np.arange(NZ)
    angle = 2 * np.pi * ((z[:, None] * z[None, :]) % NZ) / NZ
    cos, sin = np.cos(angle) / 8, np.sin(angle) / 8
    depth = np.zeros((7, 2, NZ, NZ, 16), np.float32)
    depth_back = np.zeros((NZ, 16, 7, 2, NZ), np.float32)
    for q in range(7):
        depth[q, 0, :, :, 2 * q] = cos
        depth[q, 0, :, :, 2 * q + 1] = sin
        depth[q, 1, :, :, 2 * q] = -sin
        depth[q, 1, :, :, 2 * q + 1] = cos
        depth_back[:, 2 * q, q, 0] = cos
        depth_back[:, 2 * q, q, 1] = -sin
        depth_back[:, 2 * q + 1, q, 0] = sin
        depth_back[:, 2 * q + 1, q, 1] = cos
    depth = depth.reshape(896, 1024)
    depth_back = depth_back.reshape(1024, 896)
    spread = np.zeros((384, 20, 128), np.float32)
    for shift in range(-9, 10):
        for j in range(3):
            for comp in range(10):
                other = comp + shift
                if 0 <= other < 10:
                    first = j * 40 + comp * 4
                    spread[j * 128 + comp * 10 + other, shift + 9, first : first + 4] = 1
    spread = spread.reshape(384, 2560)
    out = (expand_u, expand_s, collect, rows, rows_back, depth, depth_back, spread)
    return tuple(t.astype(half) for t in out)


def dot(a, b, dims=NN):
    return lax.dot_general(a, b, dims, preferred_element_type=F32)


def main_kernel(*refs):
    sources, refs = refs[:17], refs[17:]
    grad_ref, sums_mid_ref, sums_small_ref = refs[:3]
    held, refs = refs[3:20], refs[20:]
    (
        up_ref, s_ref, eu_ref, es_ref, rows_t, image_ref, w1_ref, w2_ref, w3_ref, w4_ref, w5_ref,
        k_ref, spread_t, depth_t, depth_back_t, eo_ref, rows_back_t,
    ) = held
    (
        taps_ref, coil, maps, message, arrived, mixed, message_back, returned, unpacked, coefs,
        direct, up_rows, padded, stage_image, stage_delta, packed_image, packed_delta, acts, slopes,
        deltas, inside, back_core, back_rows, parts_mid, parts_small, halves_mid, halves_small,
        folded_mid, folded_small, gathered_mid, gathered_small, gathered_first, own_mid, own_small, across_mid,
        across_small, total_mid, total_small, table_sem, send_sem, recv_sem, block_send, block_recv,
        sum_send, sum_recv,
    ) = refs
    subj = lax.axis_index("subj")
    slab = lax.axis_index("slab")
    z_hi, core = subj // 2, subj % 2
    z_lo, place = slab // 16, slab % 16
    plane_index = core * 16 + place
    depth_index = z_hi * 4 + z_lo

    def slab_peer(step):
        return (subj, lax.rem(slab + step, SLABS))

    def plane_peer(step):
        other = lax.rem(place + step, 16)
        return other, (subj, z_lo * 16 + other)

    def both_peer(step):
        other = lax.rem(plane_index + step, 32)
        return other, (z_hi * 2 + other // 16, z_lo * 16 + other % 16)

    twin = (z_hi * 2 + 1 - core, slab)

    def depth_peer(step):
        other = lax.rem(depth_index + step, 8)
        return other, ((other // 4) * 2 + core, (other % 4) * 16 + place)

    z_block, y_block = slab // 8, slab % 8
    zero_planes = jnp.zeros((8, 32, 128), BF16)
    for first, edge in ((0, 0), (16, 7)):

        @pl.when(z_block == edge)
        def _(first=first):
            packed_image[first : first + 8] = zero_planes
            packed_delta[first : first + 8] = zero_planes

    barrier = pltpu.get_barrier_semaphore()

    def greet(device):
        pl.semaphore_signal(barrier, inc=1, device_id=device, device_id_type=MESH)

    @pl.loop(1, SLABS)
    def _(step):
        greet(slab_peer(step))

    @pl.loop(0, 16)
    def _(other):
        greet((z_hi * 2 + 1 - core, z_lo * 16 + other))

    @pl.loop(0, 4)
    def _(other):
        greet(((1 - z_hi) * 2 + core, other * 16 + place))

    fetches = [
        pltpu.make_async_copy(source, target, table_sem.at[i])
        for i, (source, target) in enumerate(zip(sources, held))
    ]
    for fetch in fetches[:5]:
        fetch.start()

    for i in range(3):
        parts_mid[i, 28:32] = jnp.zeros((4, 32, 128), BF16)
    for i in range(2):
        parts_small[i, 21:32] = jnp.zeros((11, 16, 128), BF16)
    def cut(block, stage):
        padded[8 : 8 + NY, :] = block
        for piece in range(8):
            upper = padded[40 * piece : 40 * piece + 32, :]
            lower = padded[40 * piece + 32 : 40 * piece + 64, :]
            stage[piece] = (upper + pltpu.roll(lower, 32, 1)).astype(BF16)

    def unpack(source, target):
        block = source[...]
        lower = pltpu.roll(block.astype(F32).reshape(24 * 32, 128), 96, 1).astype(BF16)
        target[:, 0:32] = block
        target[:, 32:64] = lower.reshape(24, 32, 128)

    padded[0:8, :] = jnp.zeros((8, 128), F32)
    padded[8 + NY :, :] = jnp.zeros((16, 128), F32)

    def blocks_send(stage, target, which):
        for group, step in ((1, -1), (2, 1), (0, 0)):
            other_block = jnp.clip(z_block + step, 0, 7)
            slot = y_block + 8 - 8 * step

            @pl.when(z_block + step == other_block)
            def _():
                @pl.loop(0 if step else 1, 8)
                def _(turn):
                    piece = lax.rem(y_block + turn, 8)
                    pltpu.make_async_remote_copy(
                        stage.at[piece], target.at[slot],
                        block_send.at[which, group], block_recv.at[which, group],
                        (subj, other_block * 8 + piece), MESH,
                    ).start()

        target[y_block + 8] = stage[y_block]

    def blocks_wait(stage, target, which):
        bulk_wait(stage, 7, block_send.at[which, 0])
        bulk_wait(target, 7, block_recv.at[which, 0])

        @pl.when(z_block > 0)
        def _():
            bulk_wait(stage, 8, block_send.at[which, 1])
            bulk_wait(target, 8, block_recv.at[which, 2])

        @pl.when(z_block < 7)
        def _():
            bulk_wait(stage, 8, block_send.at[which, 2])
            bulk_wait(target, 8, block_recv.at[which, 1])

    def exchange_start(source, target, which):
        @pl.loop(1, SLABS)
        def _(step):
            subject, other = slab_peer(step)
            pltpu.make_async_remote_copy(
                source.at[other], target.at[slab], send_sem.at[which], recv_sem.at[which],
                (subject, other), MESH,
            ).start()

        target[slab] = source[slab]

    def bulk_wait(buffer, count, semaphore):
        piece = buffer.at[pl.ds(0, count)]
        pltpu.make_async_copy(piece, piece, semaphore).wait()

    def exchange_wait(source, target, which):
        bulk_wait(source, SLABS - 1, send_sem.at[which])
        bulk_wait(target, SLABS - 1, recv_sem.at[which])

    for fetch in fetches[:4]:
        fetch.wait()
    lane = lax.broadcasted_iota(jnp.int32, (20, 128), 1)
    channel = lax.broadcasted_iota(jnp.int32, (20, 128), 0)
    places = [jnp.where(lane == x * 64 + channel, 1.0, 0.0).astype(BF16) for x in range(2)]
    u_high = [up_ref[:, x, :].astype(BF16) for x in range(2)]
    s_high = [s_ref[:, x, :].astype(BF16) for x in range(2)]
    wide_u = dot(eu_ref[0], u_high[0]) + dot(eu_ref[1], u_high[1])
    wide_s = dot(es_ref[0], s_high[0]) + dot(es_ref[1], s_high[1])
    u_re, u_im = wide_u[:256], wide_u[256:]
    s_re, s_im = wide_s[:256], wide_s[256:]
    coil[...] = jnp.zeros((256, 768), BF16)
    coil[:, 0:NY] = (s_re * u_re - s_im * u_im).astype(BF16)
    coil[:, 384 : 384 + NY] = (s_re * u_im + s_im * u_re).astype(BF16)
    fetches[4].wait()
    for fetch in fetches[5:]:
        fetch.start()
    sub = lax.broadcasted_iota(jnp.int32, (8, 8, 128), 1) // 2

    @pl.loop(0, 8)
    def _(step):
        first = pl.multiple_of(step * 128, 128)
        spectra = dot(rows_t[pl.ds(first, 128), :], coil[...], NT)
        body = spectra[:, :128].reshape(8, 2, 8, 128)
        rest = spectra[:, 128:].reshape(8, 2, 8, 128)
        low, high = rest[:, 0], rest[:, 1]
        lowered = pltpu.roll(low, 6, 1)
        at_one = pltpu.roll(low, 2, 1) + pltpu.roll(low, 40, 2) + pltpu.roll(lowered, 80, 2)
        at_two = lowered + pltpu.roll(pltpu.roll(high, 4, 1), 40, 2)
        extra = jnp.where(sub == 1, at_one, jnp.where(sub == 2, at_two, 0.0))
        packed = jnp.concatenate([body[:, 0:1], (body[:, 1] + extra)[:, None]], axis=1)
        message[pl.ds(step * 8, 8)] = packed.reshape(8, 16, 128).astype(BF16)

    def three_planes(buffer, first, count):
        pieces = [buffer[first + k : first + k + count].reshape(count * 64, 128) for k in (-1, 0, 1)]
        return jnp.concatenate(pieces, axis=1)

    def ranges(low, high):
        return [(first, min(STEP, high - first)) for first in range(low, high, STEP)]

    def forward(level):
        taps = taps_ref[level]
        if level == 0:
            wide = jnp.concatenate(
                [jnp.concatenate([taps[3 * k + j] for j in range(3)], axis=1) for k in range(3)],
                axis=0,
            )
        else:
            wide = jnp.concatenate(
                [taps[3 * k : 3 * k + 3].reshape(384, 128) for k in range(3)], axis=1
            )
        for first, count in ranges(level + 1, 23 - level):
            out = dot(three_planes(acts.at[level], first, count), wide, NN if level == 0 else NT)
            rows = count * 64
            pre = (
                pltpu.roll(out[:, :128], 1, 0)
                + out[:, 128:256]
                + pltpu.roll(out[:, 256:], rows - 1, 0)
            )
            keep = inside[first : first + count].reshape(rows, 128)
            sigmoid = jax.nn.sigmoid(pre) * keep
            value = pre * sigmoid
            slope = sigmoid + value * (1.0 - jax.nn.sigmoid(pre))
            acts[level + 1, first : first + count] = value.astype(BF16).reshape(count, 64, 128)
            slopes[level, first : first + count] = slope.reshape(count, 64, 128)

    fetches[5].wait()
    image = image_ref[...].astype(F32)
    cut(
        sum(dot(image[:, x, :].astype(BF16), places[x], TN) for x in range(2)), stage_image
    )
    pl.semaphore_wait(barrier, 83)
    exchange_start(message, arrived, 0)
    blocks_send(stage_image, packed_image, 0)
    crossed = (((0,), (1,)), ((), ()))
    maps[...] = dot(s_high[0], es_ref[0], crossed) + dot(s_high[1], es_ref[1], crossed)
    rows_sum = jnp.zeros((NY, 128), F32)
    for x in range(2):
        low = (up_ref[:, x, :] - u_high[x].astype(F32)).astype(BF16)
        rows_sum += dot(u_high[x], places[x], TN) + dot(low, places[x], TN)
    up_rows[...] = rows_sum
    for fetch in fetches[6:12]:
        fetch.wait()
    for level, w_ref in enumerate((w1_ref, w2_ref, w3_ref, w4_ref, w5_ref)):
        for tap in range(9):
            low, middle, high = [
                w_ref[(tap // 3) * 9 + off_x * 3 + tap % 3].astype(F32) for off_x in range(3)
            ]
            if level == 0:
                low, high = high, low
            pieces = [jnp.concatenate(pair, axis=1) for pair in ((middle, high), (low, middle))]
            if level in (0, 4):
                pieces = [
                    jnp.concatenate([piece, jnp.zeros((44, 128), F32)], axis=0) for piece in pieces
                ]
            taps_ref[level, tap] = jnp.concatenate(pieces, axis=0).astype(BF16)

    slot_z = lax.broadcasted_iota(jnp.int32, (24, 64, 128), 0) + (z_block * 8 - 8)
    slot_y = lax.broadcasted_iota(jnp.int32, (24, 64, 128), 1) + (y_block * 40 - 8)
    grid_ok = (slot_z >= 0) & (slot_z < NZ) & (slot_y >= 0) & (slot_y < NY)
    inside[...] = jnp.where(grid_ok, 1.0, 0.0)

    fetches[12].wait()
    columns = []
    for q in range(7):
        rows = []
        for j in range(3):
            ky, x = slot_block(q, j)
            rows += [k_ref[:, ky, x, :], jnp.zeros((28, NZ), F32)]
        columns.append(jnp.concatenate(rows, axis=0))
    stacked = jnp.concatenate(columns, axis=1).astype(BF16)
    for step in range(10):
        pair = dot(stacked, spread_t[:, step * 256 : step * 256 + 256], TN)
        coefs[2 * step] = pair[:, :128]
        if step < 9:
            coefs[2 * step + 1] = pair[:, 128:]

    fetches[13].wait()
    fetches[14].wait()
    exchange_wait(message, arrived, 0)

    for q in range(7):
        first = q * 128
        spectrum = dot(depth_t[pl.ds(first, 128), :], arrived[...].reshape(1024, 128))
        real, imag = spectrum[:64], spectrum[64:]
        out_real = jnp.zeros((64, 128), F32)
        out_imag = jnp.zeros((64, 128), F32)
        for shift in range(-9, 10):
            factor = coefs[shift + 9, q * 64 : q * 64 + 64, :]
            turn = (-4 * shift) % 128
            moved_real = real if turn == 0 else pltpu.roll(real, turn, 1)
            moved_imag = imag if turn == 0 else pltpu.roll(imag, turn, 1)
            out_real += factor * moved_real
            out_imag += factor * moved_imag
        mixed[pl.ds(first, 64), :] = out_real.astype(BF16)
        mixed[pl.ds(first + 64, 64), :] = out_imag.astype(BF16)

    for step in range(2):
        first = step * 512
        back = dot(depth_back_t[pl.ds(first, 512), :], mixed[...])
        message_back[pl.ds(step * 32, 32)] = back.astype(BF16).reshape(32, 16, 128)

    exchange_start(message_back, returned, 1)
    blocks_wait(stage_image, packed_image, 0)
    unpack(packed_image, acts.at[0])
    for level in range(4):
        forward(level)
    exchange_wait(message_back, returned, 1)

    @pl.loop(0, 8)
    def _(step):
        block = returned[pl.ds(step * 8, 8)].astype(F32)
        body = block.reshape(8, 2, 8, 128)[:, 1]
        raised = pltpu.roll(body, 2, 1)
        low = jnp.where(
            sub == 0,
            pltpu.roll(body, 6, 1),
            jnp.where(
                sub == 1,
                pltpu.roll(body, 88, 2),
                jnp.where(sub == 2, pltpu.roll(raised, 48, 2), raised),
            ),
        )
        high = jnp.where(sub == 0, pltpu.roll(pltpu.roll(body, 4, 1), 88, 2), 0.0)
        rest = jnp.concatenate([low[:, None], high[:, None]], axis=1).reshape(128, 128)
        first = pl.multiple_of(step * 128, 128)
        unpacked[pl.ds(first, 128), 0:128] = block.reshape(128, 128).astype(BF16)
        unpacked[pl.ds(first, 128), 128:256] = rest.astype(BF16)

    fetches[15].wait()
    fetches[16].wait()
    back_re = dot(rows_back_t[0:NY, :], unpacked[...])
    back_im = dot(rows_back_t[NY:, :], unpacked[...])
    s_re, s_im = maps[:, :256], maps[:, 256:]
    out_re = (s_re * back_re + s_im * back_im).astype(BF16)
    out_im = (s_re * back_im - s_im * back_re).astype(BF16)
    normal = dot(out_re, eo_ref[0:256, :]) + dot(out_im, eo_ref[256:, :])
    own_direct = up_rows[...] - 0.5 * normal
    direct[...] = own_direct
    cut(own_direct, stage_delta)
    blocks_send(stage_delta, packed_delta, 1)

    def buffers_of(level):
        if level in (0, 4):
            every = (
                parts_small, halves_small, folded_small, gathered_small, own_small,
                across_small, total_small,
            )
            return [buffer.at[level // 4] for buffer in every]
        every = (
            parts_mid, halves_mid, folded_mid, gathered_mid, own_mid, across_mid, total_mid,
        )
        return [buffer.at[level - 1] for buffer in every]

    def halves_copy(level):
        parts, halves = buffers_of(level)[:2]
        return pltpu.make_async_remote_copy(
            parts.at[pl.ds(16 * (1 - core), 16)], halves,
            sum_send.at[level, 0], sum_recv.at[level, 0], twin, MESH,
        )

    def sum_halves(level):
        if level > 0:
            halves_copy(level).start()

    def sum_scatter(level):
        parts, halves, folded, gathered = buffers_of(level)[:4]
        if level == 0:

            @pl.loop(1, 32)
            def _(step):
                other, device = both_peer(step)
                pltpu.make_async_remote_copy(
                    parts.at[other], gathered_first.at[plane_index],
                    sum_send.at[level, 1], sum_recv.at[level, 1], device, MESH,
                ).start()

            gathered_first[plane_index] = parts[plane_index]
            return
        halves_copy(level).wait()
        mine = parts[pl.ds(16 * core, 16)].astype(F32)
        folded[...] = (mine + halves[...].astype(F32)).astype(BF16)

        @pl.loop(1, 16)
        def _(step):
            other, device = plane_peer(step)
            pltpu.make_async_remote_copy(
                folded.at[other], gathered.at[place],
                sum_send.at[level, 1], sum_recv.at[level, 1], device, MESH,
            ).start()

        gathered[place] = folded[place]

    def sum_across(level):
        _, _, folded, gathered, own, across, _ = buffers_of(level)
        if level == 0:
            folded = gathered = gathered_first
        count = 31 if level == 0 else 15
        bulk_wait(folded, count, sum_send.at[level, 1])
        bulk_wait(gathered, count, sum_recv.at[level, 1])
        own[0] = jnp.sum(gathered[...].astype(F32), axis=0).astype(BF16)

        @pl.loop(1, 8)
        def _(step):
            _, device = depth_peer(step)
            pltpu.make_async_remote_copy(
                own.at[0], across.at[depth_index],
                sum_send.at[level, 2], sum_recv.at[level, 2], device, MESH,
            ).start()

        across[depth_index] = own[0]

    def sum_spread(level):
        across, total = buffers_of(level)[5:]
        bulk_wait(across, 7, sum_send.at[level, 2])
        bulk_wait(across, 7, sum_recv.at[level, 2])
        total[plane_index] = jnp.sum(across[...].astype(F32), axis=0).astype(BF16)

        @pl.loop(1, 32)
        def _(step):
            _, device = both_peer(step)
            pltpu.make_async_remote_copy(
                total.at[plane_index], total.at[plane_index],
                sum_send.at[level, 3], sum_recv.at[level, 3], device, MESH,
            ).start()

    def sum_finish(level):
        total = buffers_of(level)[6]
        bulk_wait(total, 31, sum_send.at[level, 3])
        bulk_wait(total, 31, sum_recv.at[level, 3])
        if level in (0, 4):
            sums_small_ref[level // 4] = total[...].reshape(512, 128)
        else:
            sums_mid_ref[level - 1] = total[...].reshape(1024, 128)

    def weight_part(level):
        parts = buffers_of(level)[0]
        delta = deltas[level, 8:16].astype(F32).reshape(512, 128)
        row = lax.broadcasted_iota(jnp.int32, (512, 128), 0) % 64
        delta = jnp.where((row >= 8) & (row < 48), delta, 0.0)
        moved = jnp.concatenate(
            [pltpu.roll(delta, 511, 0), delta, pltpu.roll(delta, 1, 0)], axis=1
        ).astype(BF16)
        inputs = three_planes(acts.at[level], 8, 8)
        if level == 0:
            raw = dot(inputs, moved, TN)
        else:
            raw = dot(moved, inputs, TN)
        count = 24 if level in (0, 4) else 64
        lane = lax.broadcasted_iota(jnp.int32, (count, 128), 1)
        slots, lower, turned = [], [], []
        for a in range(3):
            for b in range(3):
                first = raw[a * 128 : a * 128 + count, b * 128 : b * 128 + 128]
                second = raw[a * 128 + 64 : a * 128 + 64 + count, b * 128 : b * 128 + 128]
                roll = pltpu.roll(second, 64, 1)
                slots.append(first + jnp.where(lane < 64, roll, 0.0))
                lower.append(second)
                turned.append(roll)
        for k in range(5):
            left = lower[2 * k + 1] if k < 4 else jnp.zeros((count, 128), F32)
            slots.append(jnp.where(lane < 64, left, turned[2 * k]))
        if count == 64:
            for k in range(14):
                parts[2 * k : 2 * k + 2] = slots[k].astype(BF16).reshape(2, 32, 128)
        else:
            for k in range(7):
                both = jnp.concatenate([slots[2 * k], slots[2 * k + 1]], axis=0)
                parts[3 * k : 3 * k + 3] = both.astype(BF16).reshape(3, 16, 128)

    blocks_wait(stage_delta, packed_delta, 1)
    unpack(packed_delta, deltas.at[4])
    for level in (4, 3, 2, 1, 0):
        weight_part(level)
        sum_halves(level)
        taps = taps_ref[level]
        if level == 0:
            wide = jnp.concatenate(
                [jnp.concatenate([taps[3 * k + j] for k in (2, 1, 0)], axis=1) for j in range(3)],
                axis=0,
            )
        else:
            wide = jnp.concatenate(
                [jnp.concatenate([taps[3 * k + j] for j in range(3)], axis=1) for k in (2, 1, 0)],
                axis=0,
            )
        for first, count in ranges(8 - level, 16 + level):
            out = dot(three_planes(deltas.at[level], first, count), wide, NT if level == 0 else NN)
            rows = count * 64
            back = (
                pltpu.roll(out[:, :128], rows - 1, 0)
                + out[:, 128:256]
                + pltpu.roll(out[:, 256:], 1, 0)
            ).reshape(count, 64, 128)
            if level > 0:
                slope = slopes[level - 1, first : first + count]
                deltas[level - 1, first : first + count] = (back * slope).astype(BF16)
            else:
                back_core[first - 8 : first - 8 + count] = back[:, 8:48]
        sum_scatter(level)
        if level == 0:
            sum_across(4)

    @pl.loop(1, 8)
    def _(turn):
        other = lax.rem(y_block + turn, 8)
        pltpu.make_async_remote_copy(
            back_core.at[other], back_rows.at[y_block],
            block_send.at[2, 0], block_recv.at[2, 0], (subj, z_block * 8 + other), MESH,
        ).start()

    back_rows[y_block] = back_core[y_block]
    sum_across(3)
    sum_across(2)
    sum_across(1)
    sum_spread(4)
    sum_across(0)
    for level in (3, 2, 1, 0):
        sum_spread(level)
    bulk_wait(back_core, 7, block_send.at[2, 0])
    bulk_wait(back_rows, 7, block_recv.at[2, 0])
    grad_ref[...] = direct[...] + back_rows[...].reshape(NY, 128)
    for level in (4, 3, 2, 1, 0):
        sum_finish(level)


def main_call(up, s, image, weights, kernel):
    eu, es, eo, rows, rows_back, depth, depth_back, spread = tables()
    vmem = pl.BlockSpec(memory_space=pltpu.VMEM)
    sources = [
        up, s, eu, es, rows, image, *weights, kernel, spread, depth, depth_back, eo, rows_back
    ]
    return pl.pallas_call(
        main_kernel,
        out_shape=(
            jax.ShapeDtypeStruct((NY, 128), F32),
            jax.ShapeDtypeStruct((3, 1024, 128), BF16),
            jax.ShapeDtypeStruct((2, 512, 128), BF16),
        ),
        in_specs=[pl.BlockSpec(memory_space=pl.ANY)] * len(sources),
        out_specs=(vmem, vmem, vmem),
        scratch_shapes=[pltpu.VMEM(t.shape, t.dtype) for t in sources]
        + [
            pltpu.VMEM((5, 9, 128, 128), BF16),
            pltpu.VMEM((256, 768), BF16),
            pltpu.VMEM((NY, 512), F32),
            pltpu.VMEM((SLABS, 16, 128), BF16),
            pltpu.VMEM((SLABS, 16, 128), BF16),
            pltpu.VMEM((896, 128), BF16),
            pltpu.VMEM((SLABS, 16, 128), BF16),
            pltpu.VMEM((SLABS, 16, 128), BF16),
            pltpu.VMEM((1024, 256), BF16),
            pltpu.VMEM((19, 448, 128), F32),
            pltpu.VMEM((NY, 128), F32),
            pltpu.VMEM((NY, 128), F32),
            pltpu.VMEM((NY + 24, 128), F32),
            pltpu.VMEM((8, 32, 128), BF16),
            pltpu.VMEM((8, 32, 128), BF16),
            pltpu.VMEM((24, 32, 128), BF16),
            pltpu.VMEM((24, 32, 128), BF16),
            pltpu.VMEM((5, 24, 64, 128), BF16),
            pltpu.VMEM((4, 24, 64, 128), F32),
            pltpu.VMEM((5, 24, 64, 128), BF16),
            pltpu.VMEM((24, 64, 128), F32),
            pltpu.VMEM((8, 40, 128), F32),
            pltpu.VMEM((8, 40, 128), F32),
            pltpu.VMEM((3, 32, 32, 128), BF16),
            pltpu.VMEM((2, 32, 16, 128), BF16),
        ]
        + [
            pltpu.VMEM(shape, BF16)
            for _ in range(3)
            for shape in ((3, 16, 32, 128), (2, 16, 16, 128))
        ]
        + [
            pltpu.VMEM((32, 16, 128), BF16),
            pltpu.VMEM((3, 1, 32, 128), BF16),
            pltpu.VMEM((2, 1, 16, 128), BF16),
            pltpu.VMEM((3, 8, 32, 128), BF16),
            pltpu.VMEM((2, 8, 16, 128), BF16),
            pltpu.VMEM((3, 32, 32, 128), BF16),
            pltpu.VMEM((2, 32, 16, 128), BF16),
            pltpu.SemaphoreType.DMA((17,)),
            pltpu.SemaphoreType.DMA((2,)),
            pltpu.SemaphoreType.DMA((2,)),
            pltpu.SemaphoreType.DMA((3, 3)),
            pltpu.SemaphoreType.DMA((3, 3)),
            pltpu.SemaphoreType.DMA((5, 5)),
            pltpu.SemaphoreType.DMA((5, 5)),
        ],
        compiler_params=pltpu.CompilerParams(
            collective_id=0, has_side_effects=True, vmem_limit_bytes=60 * 1024 * 1024
        ),
        cost_estimate=pl.CostEstimate(
            flops=8_000_000_000, bytes_accessed=20_000_000, transcendentals=400_000
        ),
        name="step",
    )(*sources)


def finish_kernel(scale, mid_ref, small_ref, first_ref, second_ref, third_ref, fourth_ref, last_ref):
    def place(source, count, keep, target, tap_of):
        def rows_at(slot):
            if count == 64:
                return source[slot * 64 : slot * 64 + 64, :].astype(F32)
            start = (slot // 2) * 48
            both = source[start : start + 48, :].astype(F32)
            return both[(slot % 2) * 24 : (slot % 2) * 24 + 24]

        def left(block):
            return block[:keep, :64] * scale

        def right(block):
            return pltpu.roll(block, 64, 1)[:keep, :64] * scale

        for a in range(3):
            for b in range(3):
                block = rows_at(a * 3 + b)
                target[tap_of(a, b, 0)] = left(block)
                target[tap_of(a, b, 1)] = right(block)
        for k in range(5):
            block = rows_at(9 + k)
            target[tap_of((2 * k) // 3, (2 * k) % 3, 2)] = right(block)
            if k < 4:
                target[tap_of((2 * k + 1) // 3, (2 * k + 1) % 3, 2)] = left(block)

    def usual(a, b, kind):
        return b * 9 + (1, 2, 0)[kind] * 3 + a

    def turned(a, b, kind):
        return a * 9 + (1, 0, 2)[kind] * 3 + b

    place(small_ref.at[0], 24, 20, first_ref, turned)
    place(mid_ref.at[0], 64, 64, second_ref, usual)
    place(mid_ref.at[1], 64, 64, third_ref, usual)
    place(mid_ref.at[2], 64, 64, fourth_ref, usual)
    place(small_ref.at[1], 24, 20, last_ref, usual)


def finish_call(mid, small, cells):
    shapes = [(27, 20, 64), (27, 64, 64), (27, 64, 64), (27, 64, 64), (27, 20, 64)]
    return pl.pallas_call(
        functools.partial(finish_kernel, 1.0 / math.sqrt(cells)),
        out_shape=[jax.ShapeDtypeStruct(shape, F32) for shape in shapes],
        in_specs=[pl.BlockSpec(memory_space=pltpu.VMEM)] * 2,
        out_specs=[pl.BlockSpec(memory_space=pltpu.VMEM)] * 5,
        compiler_params=pltpu.CompilerParams(vmem_limit_bytes=24 * 1024 * 1024),
        name="finish",
    )(mid, small)


def body(image, upstream, coil_maps, kernel, w_first, w_second, w_third, w_fourth, w_last):
    weights = (
        jnp.swapaxes(w_first.reshape(27, 64, 20), 1, 2),
        w_second.reshape(27, 64, 64),
        w_third.reshape(27, 64, 64),
        w_fourth.reshape(27, 64, 64),
        w_last.reshape(27, 20, 64),
    )
    bands = jnp.transpose(kernel, (0, 1, 4, 3, 2)).reshape(100, 5, 2, NZ)
    grad, mid, small = main_call(
        upstream[0, :, 0], coil_maps[0].reshape(16, 2, NY), image[0, :, 0], weights, bands
    )
    cells = (
        lax.axis_size("subj") * image.shape[0] * lax.axis_size("slab") * image.shape[2] * 2 * NY
    )
    first, second, third, fourth, last = finish_call(mid, small, cells)
    image_grad = jnp.transpose(grad.reshape(NY, 2, 64)[:, :, :20], (2, 1, 0))[None, :, None]
    return (
        image_grad,
        jnp.swapaxes(first, 1, 2).reshape(3, 3, 3, 64, 20),
        second.reshape(3, 3, 3, 64, 64),
        third.reshape(3, 3, 3, 64, 64),
        fourth.reshape(3, 3, 3, 64, 64),
        last.reshape(3, 3, 3, 20, 64),
    )


def solution(mesh):
    in_specs = (
        P("subj", None, "slab", None, None),
        P("subj", None, "slab", None, None),
        P("subj", None, None, "slab", None, None),
        P(None, None, None, None, "slab"),
        P(),
        P(),
        P(),
        P(),
        P(),
    )
    out_specs = (P("subj", None, "slab", None, None), P(), P(), P(), P(), P())
    return jax.shard_map(body, mesh=mesh, in_specs=in_specs, out_specs=out_specs, check_vma=False)
```

```python
import functools
import math

import jax
import jax.numpy as jnp
import ml_dtypes
import numpy as np
from jax import lax
from jax.experimental import pallas as pl
from jax.experimental.pallas import tpu as pltpu
from jax.sharding import PartitionSpec as P

F32 = jnp.float32
BF16 = jnp.bfloat16
MESH = pl.DeviceIdType.MESH
NN = (((1,), (0,)), ((), ()))
NT = (((1,), (1,)), ((), ()))
TN = (((0,), (0,)), ((), ()))
SLABS = 64
NY = 320
NZ = 64
STEP = 8


def lane_of(x, comp, coil):
    group = x * 2 + coil // 4
    base = group * 40 if group < 3 else 128
    return base + comp * 4 + coil % 4


def slot_block(q, j):
    if q < 5:
        return q, j // 2
    if q == 5:
        return j, 1
    return min(3 + j, 4), 1


@functools.lru_cache(None)
def tables():
    half = ml_dtypes.bfloat16
    expand_u = np.zeros((2, 512, 20), np.float32)
    expand_s = np.zeros((2, 512, 16), np.float32)
    collect = np.zeros((512, 128), np.float32)
    for x in range(2):
        for comp in range(10):
            for coil in range(8):
                lane = lane_of(x, comp, coil)
                for part in range(2):
                    expand_u[x, part * 256 + lane, part * 10 + comp] = 1
                    expand_s[x, part * 256 + lane, part * 8 + coil] = 1
                    collect[part * 256 + lane, x * 64 + part * 10 + comp] = 1
    y = np.arange(NY)
    angle = 2 * np.pi * ((y[:, None] * y[None, :]) % NY) / NY
    cos = (np.cos(angle) / math.sqrt(NY)).reshape(SLABS, 5, NY)
    sin = (np.sin(angle) / math.sqrt(NY)).reshape(SLABS, 5, NY)
    rows = np.zeros((SLABS, 16, 2, 384), np.float32)
    rows[:, 0:10:2, 0, :NY] = cos
    rows[:, 0:10:2, 1, :NY] = sin
    rows[:, 1:10:2, 0, :NY] = -sin
    rows[:, 1:10:2, 1, :NY] = cos
    rows = rows.reshape(1024, 768)
    rows_back = np.zeros((2, NY, SLABS, 16), np.float32)
    cos_t, sin_t = np.moveaxis(cos, 2, 0), np.moveaxis(sin, 2, 0)
    rows_back[0, :, :, 0:10:2] = cos_t
    rows_back[0, :, :, 1:10:2] = -sin_t
    rows_back[1, :, :, 0:10:2] = sin_t
    rows_back[1, :, :, 1:10:2] = cos_t
    rows_back = rows_back.reshape(640, 1024)
    z = np.arange(NZ)
    angle = 2 * np.pi * ((z[:, None] * z[None, :]) % NZ) / NZ
    cos, sin = np.cos(angle) / 8, np.sin(angle) / 8
    depth = np.zeros((7, 2, NZ, NZ, 16), np.float32)
    depth_back = np.zeros((NZ, 16, 7, 2, NZ), np.float32)
    for q in range(7):
        depth[q, 0, :, :, 2 * q] = cos
        depth[q, 0, :, :, 2 * q + 1] = sin
        depth[q, 1, :, :, 2 * q] = -sin
        depth[q, 1, :, :, 2 * q + 1] = cos
        depth_back[:, 2 * q, q, 0] = cos
        depth_back[:, 2 * q, q, 1] = -sin
        depth_back[:, 2 * q + 1, q, 0] = sin
        depth_back[:, 2 * q + 1, q, 1] = cos
    depth = depth.reshape(896, 1024)
    depth_back = depth_back.reshape(1024, 896)
    spread = np.zeros((384, 20, 128), np.float32)
    for shift in range(-9, 10):
        for j in range(3):
            for comp in range(10):
                other = comp + shift
                if 0 <= other < 10:
                    first = j * 40 + comp * 4
                    spread[j * 128 + comp * 10 + other, shift + 9, first : first + 4] = 1
    spread = spread.reshape(384, 2560)
    out = (expand_u, expand_s, collect, rows, rows_back, depth, depth_back, spread)
    return tuple(t.astype(half) for t in out)


def dot(a, b, dims=NN):
    return lax.dot_general(a, b, dims, preferred_element_type=F32)


def main_kernel(*refs):
    sources, refs = refs[:17], refs[17:]
    grad_ref, sums_mid_ref, sums_small_ref = refs[:3]
    held, refs = refs[3:20], refs[20:]
    (
        up_ref, s_ref, eu_ref, es_ref, rows_t, image_ref, w1_ref, w2_ref, w3_ref, w4_ref, w5_ref,
        k_ref, spread_t, depth_t, depth_back_t, eo_ref, rows_back_t,
    ) = held
    (
        taps_ref, coil, maps, message, arrived, mixed, message_back, returned, unpacked, coefs,
        direct, up_rows, padded, stage_image, stage_delta, packed_image, packed_delta, acts, slopes,
        deltas, inside, back_core, back_rows, parts_mid, parts_small, halves_mid, halves_small,
        folded_mid, folded_small, gathered_mid, gathered_small, gathered_first, own_mid, own_small, across_mid,
        across_small, total_mid, total_small, table_sem, send_sem, recv_sem, block_send, block_recv,
        sum_send, sum_recv,
    ) = refs
    subj = lax.axis_index("subj")
    slab = lax.axis_index("slab")
    z_hi, core = subj // 2, subj % 2
    z_lo, place = slab // 16, slab % 16
    plane_index = core * 16 + place
    depth_index = z_hi * 4 + z_lo

    def slab_peer(step):
        return (subj, lax.rem(slab + step, SLABS))

    def plane_peer(step):
        other = lax.rem(place + step, 16)
        return other, (subj, z_lo * 16 + other)

    def both_peer(step):
        other = lax.rem(plane_index + step, 32)
        return other, (z_hi * 2 + other // 16, z_lo * 16 + other % 16)

    twin = (z_hi * 2 + 1 - core, slab)

    def depth_peer(step):
        other = lax.rem(depth_index + step, 8)
        return other, ((other // 4) * 2 + core, (other % 4) * 16 + place)

    z_block, y_block = slab // 8, slab % 8
    zero_planes = jnp.zeros((8, 32, 128), BF16)
    for first, edge in ((0, 0), (16, 7)):

        @pl.when(z_block == edge)
        def _(first=first):
            packed_image[first : first + 8] = zero_planes
            packed_delta[first : first + 8] = zero_planes

    barrier = pltpu.get_barrier_semaphore()

    def greet(device):
        pl.semaphore_signal(barrier, inc=1, device_id=device, device_id_type=MESH)

    @pl.loop(1, SLABS)
    def _(step):
        greet(slab_peer(step))

    @pl.loop(0, 16)
    def _(other):
        greet((z_hi * 2 + 1 - core, z_lo * 16 + other))

    @pl.loop(0, 4)
    def _(other):
        greet(((1 - z_hi) * 2 + core, other * 16 + place))

    fetches = [
        pltpu.make_async_copy(source, target, table_sem.at[i])
        for i, (source, target) in enumerate(zip(sources, held))
    ]
    for fetch in fetches[:12]:
        fetch.start()

    for i in range(3):
        parts_mid[i, 28:32] = jnp.zeros((4, 32, 128), BF16)
    for i in range(2):
        parts_small[i, 21:32] = jnp.zeros((11, 16, 128), BF16)
    def cut(block, stage):
        padded[8 : 8 + NY, :] = block
        for piece in range(8):
            upper = padded[40 * piece : 40 * piece + 32, :]
            lower = padded[40 * piece + 32 : 40 * piece + 64, :]
            stage[piece] = (upper + pltpu.roll(lower, 32, 1)).astype(BF16)

    def unpack(source, target):
        block = source[...]
        lower = pltpu.roll(block.astype(F32).reshape(24 * 32, 128), 96, 1).astype(BF16)
        target[:, 0:32] = block
        target[:, 32:64] = lower.reshape(24, 32, 128)

    padded[0:8, :] = jnp.zeros((8, 128), F32)
    padded[8 + NY :, :] = jnp.zeros((16, 128), F32)

    def blocks_send(stage, target, which):
        for group, step in ((1, -1), (2, 1), (0, 0)):
            other_block = jnp.clip(z_block + step, 0, 7)
            slot = y_block + 8 - 8 * step

            @pl.when(z_block + step == other_block)
            def _():
                @pl.loop(0 if step else 1, 8)
                def _(turn):
                    piece = lax.rem(y_block + turn, 8)
                    pltpu.make_async_remote_copy(
                        stage.at[piece], target.at[slot],
                        block_send.at[which, group], block_recv.at[which, group],
                        (subj, other_block * 8 + piece), MESH,
                    ).start()

        target[y_block + 8] = stage[y_block]

    def blocks_wait(stage, target, which):
        bulk_wait(stage, 7, block_send.at[which, 0])
        bulk_wait(target, 7, block_recv.at[which, 0])

        @pl.when(z_block > 0)
        def _():
            bulk_wait(stage, 8, block_send.at[which, 1])
            bulk_wait(target, 8, block_recv.at[which, 2])

        @pl.when(z_block < 7)
        def _():
            bulk_wait(stage, 8, block_send.at[which, 2])
            bulk_wait(target, 8, block_recv.at[which, 1])

    def exchange_start(source, target, which):
        @pl.loop(1, SLABS)
        def _(step):
            subject, other = slab_peer(step)
            pltpu.make_async_remote_copy(
                source.at[other], target.at[slab], send_sem.at[which], recv_sem.at[which],
                (subject, other), MESH,
            ).start()

        target[slab] = source[slab]

    def bulk_wait(buffer, count, semaphore):
        piece = buffer.at[pl.ds(0, count)]
        pltpu.make_async_copy(piece, piece, semaphore).wait()

    def exchange_wait(source, target, which):
        bulk_wait(source, SLABS - 1, send_sem.at[which])
        bulk_wait(target, SLABS - 1, recv_sem.at[which])

    for fetch in fetches[:4]:
        fetch.wait()
    lane = lax.broadcasted_iota(jnp.int32, (20, 128), 1)
    channel = lax.broadcasted_iota(jnp.int32, (20, 128), 0)
    places = [jnp.where(lane == x * 64 + channel, 1.0, 0.0).astype(BF16) for x in range(2)]
    u_high = [up_ref[:, x, :].astype(BF16) for x in range(2)]
    s_high = [s_ref[:, x, :].astype(BF16) for x in range(2)]
    wide_u = dot(eu_ref[0], u_high[0]) + dot(eu_ref[1], u_high[1])
    wide_s = dot(es_ref[0], s_high[0]) + dot(es_ref[1], s_high[1])
    u_re, u_im = wide_u[:256], wide_u[256:]
    s_re, s_im = wide_s[:256], wide_s[256:]
    coil[...] = jnp.zeros((256, 768), BF16)
    coil[:, 0:NY] = (s_re * u_re - s_im * u_im).astype(BF16)
    coil[:, 384 : 384 + NY] = (s_re * u_im + s_im * u_re).astype(BF16)
    fetches[4].wait()
    sub = lax.broadcasted_iota(jnp.int32, (8, 8, 128), 1) // 2

    @pl.loop(0, 8)
    def _(step):
        first = pl.multiple_of(step * 128, 128)
        spectra = dot(rows_t[pl.ds(first, 128), :], coil[...], NT)
        body = spectra[:, :128].reshape(8, 2, 8, 128)
        rest = spectra[:, 128:].reshape(8, 2, 8, 128)
        low, high = rest[:, 0], rest[:, 1]
        lowered = pltpu.roll(low, 6, 1)
        at_one = pltpu.roll(low, 2, 1) + pltpu.roll(low, 40, 2) + pltpu.roll(lowered, 80, 2)
        at_two = lowered + pltpu.roll(pltpu.roll(high, 4, 1), 40, 2)
        extra = jnp.where(sub == 1, at_one, jnp.where(sub == 2, at_two, 0.0))
        packed = jnp.concatenate([body[:, 0:1], (body[:, 1] + extra)[:, None]], axis=1)
        message[pl.ds(step * 8, 8)] = packed.reshape(8, 16, 128).astype(BF16)

    slot_z = lax.broadcasted_iota(jnp.int32, (24, 64, 128), 0) + (z_block * 8 - 8)
    slot_y = lax.broadcasted_iota(jnp.int32, (24, 64, 128), 1) + (y_block * 40 - 8)
    grid_ok = (slot_z >= 0) & (slot_z < NZ) & (slot_y >= 0) & (slot_y < NY)
    inside[...] = jnp.where(grid_ok, 1.0, 0.0)

    def three_planes(buffer, first, count):
        pieces = [buffer[first + k : first + k + count].reshape(count * 64, 128) for k in (-1, 0, 1)]
        return jnp.concatenate(pieces, axis=1)

    def ranges(low, high):
        return [(first, min(STEP, high - first)) for first in range(low, high, STEP)]

    def forward(level):
        taps = taps_ref[level]
        if level == 0:
            wide = jnp.concatenate(
                [jnp.concatenate([taps[3 * k + j] for j in range(3)], axis=1) for k in range(3)],
                axis=0,
            )
        else:
            wide = jnp.concatenate(
                [taps[3 * k : 3 * k + 3].reshape(384, 128) for k in range(3)], axis=1
            )
        for first, count in ranges(level + 1, 23 - level):
            out = dot(three_planes(acts.at[level], first, count), wide, NN if level == 0 else NT)
            rows = count * 64
            pre = (
                pltpu.roll(out[:, :128], 1, 0)
                + out[:, 128:256]
                + pltpu.roll(out[:, 256:], rows - 1, 0)
            )
            keep = inside[first : first + count].reshape(rows, 128)
            sigmoid = jax.nn.sigmoid(pre) * keep
            value = pre * sigmoid
            slope = sigmoid + value * (1.0 - jax.nn.sigmoid(pre))
            acts[level + 1, first : first + count] = value.astype(BF16).reshape(count, 64, 128)
            slopes[level, first : first + count] = slope.reshape(count, 64, 128)

    for fetch in fetches[12:]:
        fetch.start()
    fetches[5].wait()
    image = image_ref[...].astype(F32)
    cut(
        sum(dot(image[:, x, :].astype(BF16), places[x], TN) for x in range(2)), stage_image
    )
    crossed = (((0,), (1,)), ((), ()))
    maps[...] = dot(s_high[0], es_ref[0], crossed) + dot(s_high[1], es_ref[1], crossed)
    rows_sum = jnp.zeros((NY, 128), F32)
    for x in range(2):
        low = (up_ref[:, x, :] - u_high[x].astype(F32)).astype(BF16)
        rows_sum += dot(u_high[x], places[x], TN) + dot(low, places[x], TN)
    up_rows[...] = rows_sum
    for fetch in fetches[6:12]:
        fetch.wait()
    for level, w_ref in enumerate((w1_ref, w2_ref, w3_ref, w4_ref, w5_ref)):
        for tap in range(9):
            low, middle, high = [
                w_ref[(tap // 3) * 9 + off_x * 3 + tap % 3].astype(F32) for off_x in range(3)
            ]
            if level == 0:
                low, high = high, low
            pieces = [jnp.concatenate(pair, axis=1) for pair in ((middle, high), (low, middle))]
            if level in (0, 4):
                pieces = [
                    jnp.concatenate([piece, jnp.zeros((44, 128), F32)], axis=0) for piece in pieces
                ]
            taps_ref[level, tap] = jnp.concatenate(pieces, axis=0).astype(BF16)

    pl.semaphore_wait(barrier, 83)
    exchange_start(message, arrived, 0)
    blocks_send(stage_image, packed_image, 0)
    fetches[12].wait()
    columns = []
    for q in range(7):
        rows = []
        for j in range(3):
            ky, x = slot_block(q, j)
            rows += [k_ref[:, ky, x, :], jnp.zeros((28, NZ), F32)]
        columns.append(jnp.concatenate(rows, axis=0))
    stacked = jnp.concatenate(columns, axis=1).astype(BF16)
    for step in range(10):
        pair = dot(stacked, spread_t[:, step * 256 : step * 256 + 256], TN)
        coefs[2 * step] = pair[:, :128]
        if step < 9:
            coefs[2 * step + 1] = pair[:, 128:]

    fetches[13].wait()
    fetches[14].wait()
    exchange_wait(message, arrived, 0)

    for q in range(7):
        first = q * 128
        spectrum = dot(depth_t[pl.ds(first, 128), :], arrived[...].reshape(1024, 128))
        real, imag = spectrum[:64], spectrum[64:]
        out_real = jnp.zeros((64, 128), F32)
        out_imag = jnp.zeros((64, 128), F32)
        for shift in range(-9, 10):
            factor = coefs[shift + 9, q * 64 : q * 64 + 64, :]
            turn = (-4 * shift) % 128
            moved_real = real if turn == 0 else pltpu.roll(real, turn, 1)
            moved_imag = imag if turn == 0 else pltpu.roll(imag, turn, 1)
            out_real += factor * moved_real
            out_imag += factor * moved_imag
        mixed[pl.ds(first, 64), :] = out_real.astype(BF16)
        mixed[pl.ds(first + 64, 64), :] = out_imag.astype(BF16)

    for step in range(2):
        first = step * 512
        back = dot(depth_back_t[pl.ds(first, 512), :], mixed[...])
        message_back[pl.ds(step * 32, 32)] = back.astype(BF16).reshape(32, 16, 128)

    exchange_start(message_back, returned, 1)
    blocks_wait(stage_image, packed_image, 0)
    unpack(packed_image, acts.at[0])
    for level in range(4):
        forward(level)
    exchange_wait(message_back, returned, 1)

    @pl.loop(0, 8)
    def _(step):
        block = returned[pl.ds(step * 8, 8)].astype(F32)
        body = block.reshape(8, 2, 8, 128)[:, 1]
        raised = pltpu.roll(body, 2, 1)
        low = jnp.where(
            sub == 0,
            pltpu.roll(body, 6, 1),
            jnp.where(
                sub == 1,
                pltpu.roll(body, 88, 2),
                jnp.where(sub == 2, pltpu.roll(raised, 48, 2), raised),
            ),
        )
        high = jnp.where(sub == 0, pltpu.roll(pltpu.roll(body, 4, 1), 88, 2), 0.0)
        rest = jnp.concatenate([low[:, None], high[:, None]], axis=1).reshape(128, 128)
        first = pl.multiple_of(step * 128, 128)
        unpacked[pl.ds(first, 128), 0:128] = block.reshape(128, 128).astype(BF16)
        unpacked[pl.ds(first, 128), 128:256] = rest.astype(BF16)

    fetches[15].wait()
    fetches[16].wait()
    back_re = dot(rows_back_t[0:NY, :], unpacked[...])
    back_im = dot(rows_back_t[NY:, :], unpacked[...])
    s_re, s_im = maps[:, :256], maps[:, 256:]
    out_re = (s_re * back_re + s_im * back_im).astype(BF16)
    out_im = (s_re * back_im - s_im * back_re).astype(BF16)
    normal = dot(out_re, eo_ref[0:256, :]) + dot(out_im, eo_ref[256:, :])
    own_direct = up_rows[...] - 0.5 * normal
    direct[...] = own_direct
    cut(own_direct, stage_delta)
    blocks_send(stage_delta, packed_delta, 1)

    def buffers_of(level):
        if level in (0, 4):
            every = (
                parts_small, halves_small, folded_small, gathered_small, own_small,
                across_small, total_small,
            )
            return [buffer.at[level // 4] for buffer in every]
        every = (
            parts_mid, halves_mid, folded_mid, gathered_mid, own_mid, across_mid, total_mid,
        )
        return [buffer.at[level - 1] for buffer in every]

    def halves_copy(level):
        parts, halves = buffers_of(level)[:2]
        return pltpu.make_async_remote_copy(
            parts.at[pl.ds(16 * (1 - core), 16)], halves,
            sum_send.at[level, 0], sum_recv.at[level, 0], twin, MESH,
        )

    def sum_halves(level):
        if level > 0:
            halves_copy(level).start()

    def sum_scatter(level):
        parts, halves, folded, gathered = buffers_of(level)[:4]
        if level == 0:

            @pl.loop(1, 32)
            def _(step):
                other, device = both_peer(step)
                pltpu.make_async_remote_copy(
                    parts.at[other], gathered_first.at[plane_index],
                    sum_send.at[level, 1], sum_recv.at[level, 1], device, MESH,
                ).start()

            gathered_first[plane_index] = parts[plane_index]
            return
        halves_copy(level).wait()
        mine = parts[pl.ds(16 * core, 16)].astype(F32)
        folded[...] = (mine + halves[...].astype(F32)).astype(BF16)

        @pl.loop(1, 16)
        def _(step):
            other, device = plane_peer(step)
            pltpu.make_async_remote_copy(
                folded.at[other], gathered.at[place],
                sum_send.at[level, 1], sum_recv.at[level, 1], device, MESH,
            ).start()

        gathered[place] = folded[place]

    def sum_across(level):
        _, _, folded, gathered, own, across, _ = buffers_of(level)
        if level == 0:
            folded = gathered = gathered_first
        count = 31 if level == 0 else 15
        bulk_wait(folded, count, sum_send.at[level, 1])
        bulk_wait(gathered, count, sum_recv.at[level, 1])
        own[0] = jnp.sum(gathered[...].astype(F32), axis=0).astype(BF16)

        @pl.loop(1, 8)
        def _(step):
            _, device = depth_peer(step)
            pltpu.make_async_remote_copy(
                own.at[0], across.at[depth_index],
                sum_send.at[level, 2], sum_recv.at[level, 2], device, MESH,
            ).start()

        across[depth_index] = own[0]

    def sum_spread(level):
        across, total = buffers_of(level)[5:]
        bulk_wait(across, 7, sum_send.at[level, 2])
        bulk_wait(across, 7, sum_recv.at[level, 2])
        total[plane_index] = jnp.sum(across[...].astype(F32), axis=0).astype(BF16)
        peer = both_peer if level == 0 else plane_peer

        @pl.loop(1, 32 if level == 0 else 16)
        def _(step):
            _, device = peer(step)
            pltpu.make_async_remote_copy(
                total.at[plane_index], total.at[plane_index],
                sum_send.at[level, 3], sum_recv.at[level, 3], device, MESH,
            ).start()

    def share_copy(level):
        half = buffers_of(level)[6].at[pl.ds(16 * core, 16)]
        return pltpu.make_async_remote_copy(
            half, half, sum_send.at[level, 4], sum_recv.at[level, 4], twin, MESH
        )

    def sum_share(level):
        total = buffers_of(level)[6]
        bulk_wait(total, 15, sum_send.at[level, 3])
        bulk_wait(total, 15, sum_recv.at[level, 3])
        share_copy(level).start()

    def sum_finish(level):
        total = buffers_of(level)[6]
        if level == 0:
            bulk_wait(total, 31, sum_send.at[level, 3])
            bulk_wait(total, 31, sum_recv.at[level, 3])
        else:
            share_copy(level).wait()
        if level in (0, 4):
            sums_small_ref[level // 4] = total[...].reshape(512, 128)
        else:
            sums_mid_ref[level - 1] = total[...].reshape(1024, 128)

    def weight_part(level):
        parts = buffers_of(level)[0]
        delta = deltas[level, 8:16].astype(F32).reshape(512, 128)
        row = lax.broadcasted_iota(jnp.int32, (512, 128), 0) % 64
        delta = jnp.where((row >= 8) & (row < 48), delta, 0.0)
        moved = jnp.concatenate(
            [pltpu.roll(delta, 511, 0), delta, pltpu.roll(delta, 1, 0)], axis=1
        ).astype(BF16)
        inputs = three_planes(acts.at[level], 8, 8)
        if level == 0:
            raw = dot(inputs, moved, TN)
        else:
            raw = dot(moved, inputs, TN)
        count = 24 if level in (0, 4) else 64
        lane = lax.broadcasted_iota(jnp.int32, (count, 128), 1)
        slots, lower, turned = [], [], []
        for a in range(3):
            for b in range(3):
                first = raw[a * 128 : a * 128 + count, b * 128 : b * 128 + 128]
                second = raw[a * 128 + 64 : a * 128 + 64 + count, b * 128 : b * 128 + 128]
                roll = pltpu.roll(second, 64, 1)
                slots.append(first + jnp.where(lane < 64, roll, 0.0))
                lower.append(second)
                turned.append(roll)
        for k in range(5):
            left = lower[2 * k + 1] if k < 4 else jnp.zeros((count, 128), F32)
            slots.append(jnp.where(lane < 64, left, turned[2 * k]))
        if count == 64:
            for k in range(14):
                parts[2 * k : 2 * k + 2] = slots[k].astype(BF16).reshape(2, 32, 128)
        else:
            for k in range(7):
                both = jnp.concatenate([slots[2 * k], slots[2 * k + 1]], axis=0)
                parts[3 * k : 3 * k + 3] = both.astype(BF16).reshape(3, 16, 128)

    blocks_wait(stage_delta, packed_delta, 1)
    unpack(packed_delta, deltas.at[4])
    for level in (4, 3, 2, 1, 0):
        weight_part(level)
        sum_halves(level)
        taps = taps_ref[level]
        if level == 0:
            wide = jnp.concatenate(
                [jnp.concatenate([taps[3 * k + j] for k in (2, 1, 0)], axis=1) for j in range(3)],
                axis=0,
            )
        else:
            wide = jnp.concatenate(
                [jnp.concatenate([taps[3 * k + j] for j in range(3)], axis=1) for k in (2, 1, 0)],
                axis=0,
            )
        for first, count in ranges(8 - level, 16 + level):
            out = dot(three_planes(deltas.at[level], first, count), wide, NT if level == 0 else NN)
            rows = count * 64
            back = (
                pltpu.roll(out[:, :128], rows - 1, 0)
                + out[:, 128:256]
                + pltpu.roll(out[:, 256:], 1, 0)
            ).reshape(count, 64, 128)
            if level > 0:
                slope = slopes[level - 1, first : first + count]
                deltas[level - 1, first : first + count] = (back * slope).astype(BF16)
            else:
                back_core[first - 8 : first - 8 + count] = back[:, 8:48]
        sum_scatter(level)
        if level == 0:
            sum_across(4)

    @pl.loop(1, 8)
    def _(turn):
        other = lax.rem(y_block + turn, 8)
        pltpu.make_async_remote_copy(
            back_core.at[other], back_rows.at[y_block],
            block_send.at[2, 0], block_recv.at[2, 0], (subj, z_block * 8 + other), MESH,
        ).start()

    back_rows[y_block] = back_core[y_block]
    sum_across(3)
    sum_across(2)
    sum_across(1)
    sum_spread(4)
    sum_across(0)
    for level in (3, 2, 1, 0):
        sum_spread(level)
    bulk_wait(back_core, 7, block_send.at[2, 0])
    bulk_wait(back_rows, 7, block_recv.at[2, 0])
    grad_ref[...] = direct[...] + back_rows[...].reshape(NY, 128)
    for level in (4, 3, 2, 1):
        sum_share(level)
    for level in (4, 3, 2, 1, 0):
        sum_finish(level)


def main_call(up, s, image, weights, kernel):
    eu, es, eo, rows, rows_back, depth, depth_back, spread = tables()
    vmem = pl.BlockSpec(memory_space=pltpu.VMEM)
    sources = [
        up, s, eu, es, rows, image, *weights, kernel, spread, depth, depth_back, eo, rows_back
    ]
    return pl.pallas_call(
        main_kernel,
        out_shape=(
            jax.ShapeDtypeStruct((NY, 128), F32),
            jax.ShapeDtypeStruct((3, 1024, 128), BF16),
            jax.ShapeDtypeStruct((2, 512, 128), BF16),
        ),
        in_specs=[pl.BlockSpec(memory_space=pl.ANY)] * len(sources),
        out_specs=(vmem, vmem, vmem),
        scratch_shapes=[pltpu.VMEM(t.shape, t.dtype) for t in sources]
        + [
            pltpu.VMEM((5, 9, 128, 128), BF16),
            pltpu.VMEM((256, 768), BF16),
            pltpu.VMEM((NY, 512), F32),
            pltpu.VMEM((SLABS, 16, 128), BF16),
            pltpu.VMEM((SLABS, 16, 128), BF16),
            pltpu.VMEM((896, 128), BF16),
            pltpu.VMEM((SLABS, 16, 128), BF16),
            pltpu.VMEM((SLABS, 16, 128), BF16),
            pltpu.VMEM((1024, 256), BF16),
            pltpu.VMEM((19, 448, 128), F32),
            pltpu.VMEM((NY, 128), F32),
            pltpu.VMEM((NY, 128), F32),
            pltpu.VMEM((NY + 24, 128), F32),
            pltpu.VMEM((8, 32, 128), BF16),
            pltpu.VMEM((8, 32, 128), BF16),
            pltpu.VMEM((24, 32, 128), BF16),
            pltpu.VMEM((24, 32, 128), BF16),
            pltpu.VMEM((5, 24, 64, 128), BF16),
            pltpu.VMEM((4, 24, 64, 128), F32),
            pltpu.VMEM((5, 24, 64, 128), BF16),
            pltpu.VMEM((24, 64, 128), F32),
            pltpu.VMEM((8, 40, 128), F32),
            pltpu.VMEM((8, 40, 128), F32),
            pltpu.VMEM((3, 32, 32, 128), BF16),
            pltpu.VMEM((2, 32, 16, 128), BF16),
        ]
        + [
            pltpu.VMEM(shape, BF16)
            for _ in range(3)
            for shape in ((3, 16, 32, 128), (2, 16, 16, 128))
        ]
        + [
            pltpu.VMEM((32, 16, 128), BF16),
            pltpu.VMEM((3, 1, 32, 128), BF16),
            pltpu.VMEM((2, 1, 16, 128), BF16),
            pltpu.VMEM((3, 8, 32, 128), BF16),
            pltpu.VMEM((2, 8, 16, 128), BF16),
            pltpu.VMEM((3, 32, 32, 128), BF16),
            pltpu.VMEM((2, 32, 16, 128), BF16),
            pltpu.SemaphoreType.DMA((17,)),
            pltpu.SemaphoreType.DMA((2,)),
            pltpu.SemaphoreType.DMA((2,)),
            pltpu.SemaphoreType.DMA((3, 3)),
            pltpu.SemaphoreType.DMA((3, 3)),
            pltpu.SemaphoreType.DMA((5, 5)),
            pltpu.SemaphoreType.DMA((5, 5)),
        ],
        compiler_params=pltpu.CompilerParams(
            collective_id=0, has_side_effects=True, vmem_limit_bytes=60 * 1024 * 1024
        ),
        cost_estimate=pl.CostEstimate(
            flops=8_000_000_000, bytes_accessed=20_000_000, transcendentals=400_000
        ),
        name="step",
    )(*sources)


def finish_kernel(scale, mid_ref, small_ref, first_ref, second_ref, third_ref, fourth_ref, last_ref):
    def place(source, count, keep, target, tap_of):
        def rows_at(slot):
            if count == 64:
                return source[slot * 64 : slot * 64 + 64, :].astype(F32)
            start = (slot // 2) * 48
            both = source[start : start + 48, :].astype(F32)
            return both[(slot % 2) * 24 : (slot % 2) * 24 + 24]

        def left(block):
            return block[:keep, :64] * scale

        def right(block):
            return pltpu.roll(block, 64, 1)[:keep, :64] * scale

        for a in range(3):
            for b in range(3):
                block = rows_at(a * 3 + b)
                target[tap_of(a, b, 0)] = left(block)
                target[tap_of(a, b, 1)] = right(block)
        for k in range(5):
            block = rows_at(9 + k)
            target[tap_of((2 * k) // 3, (2 * k) % 3, 2)] = right(block)
            if k < 4:
                target[tap_of((2 * k + 1) // 3, (2 * k + 1) % 3, 2)] = left(block)

    def usual(a, b, kind):
        return b * 9 + (1, 2, 0)[kind] * 3 + a

    def turned(a, b, kind):
        return a * 9 + (1, 0, 2)[kind] * 3 + b

    place(small_ref.at[0], 24, 20, first_ref, turned)
    place(mid_ref.at[0], 64, 64, second_ref, usual)
    place(mid_ref.at[1], 64, 64, third_ref, usual)
    place(mid_ref.at[2], 64, 64, fourth_ref, usual)
    place(small_ref.at[1], 24, 20, last_ref, usual)


def finish_call(mid, small, cells):
    shapes = [(27, 20, 64), (27, 64, 64), (27, 64, 64), (27, 64, 64), (27, 20, 64)]
    return pl.pallas_call(
        functools.partial(finish_kernel, 1.0 / math.sqrt(cells)),
        out_shape=[jax.ShapeDtypeStruct(shape, F32) for shape in shapes],
        in_specs=[pl.BlockSpec(memory_space=pltpu.VMEM)] * 2,
        out_specs=[pl.BlockSpec(memory_space=pltpu.VMEM)] * 5,
        compiler_params=pltpu.CompilerParams(vmem_limit_bytes=24 * 1024 * 1024),
        name="finish",
    )(mid, small)


def body(image, upstream, coil_maps, kernel, w_first, w_second, w_third, w_fourth, w_last):
    weights = (
        jnp.swapaxes(w_first.reshape(27, 64, 20), 1, 2),
        w_second.reshape(27, 64, 64),
        w_third.reshape(27, 64, 64),
        w_fourth.reshape(27, 64, 64),
        w_last.reshape(27, 20, 64),
    )
    bands = jnp.transpose(kernel, (0, 1, 4, 3, 2)).reshape(100, 5, 2, NZ)
    grad, mid, small = main_call(
        upstream[0, :, 0], coil_maps[0].reshape(16, 2, NY), image[0, :, 0], weights, bands
    )
    cells = (
        lax.axis_size("subj") * image.shape[0] * lax.axis_size("slab") * image.shape[2] * 2 * NY
    )
    first, second, third, fourth, last = finish_call(mid, small, cells)
    image_grad = jnp.transpose(grad.reshape(NY, 2, 64)[:, :, :20], (2, 1, 0))[None, :, None]
    return (
        image_grad,
        jnp.swapaxes(first, 1, 2).reshape(3, 3, 3, 64, 20),
        second.reshape(3, 3, 3, 64, 64),
        third.reshape(3, 3, 3, 64, 64),
        fourth.reshape(3, 3, 3, 64, 64),
        last.reshape(3, 3, 3, 20, 64),
    )


def solution(mesh):
    in_specs = (
        P("subj", None, "slab", None, None),
        P("subj", None, "slab", None, None),
        P("subj", None, None, "slab", None, None),
        P(None, None, None, None, "slab"),
        P(),
        P(),
        P(),
        P(),
        P(),
    )
    out_specs = (P("subj", None, "slab", None, None), P(), P(), P(), P(), P())
    return jax.shard_map(body, mesh=mesh, in_specs=in_specs, out_specs=out_specs, check_vma=False)
```
